512 devices in a mesh: leaf: 512 (over y, z, x, core).
Axes of the slice: x: 4, y: 4, z: 16, core: 2. Of those that a mesh axis runs over, the one named last changes fastest.
Arguments:
- right_side: float32 [131072, 128], P('leaf'), may hold values from -6 to 6
- leaf_inverse: float32 [131072, 256], P('leaf'), may hold values from -1 to 3, as said below
- bases: float32 [9, 131072, 128], P(None, 'leaf'), may hold values from -5 to 5
Outputs:
- solution: float32 [131072, 128], P('leaf')
The draws below stay inside these ranges and needn't reach their ends.
Inputs may be any that keep to these rules, and one draw needn't show every extreme that they name: `leaf_inverse`: each leaf's block is a symmetric matrix with a positive diagonal; for every node and level, the singular values of I - G_o G_w lie between 0.5 and 1.5.
All inputs are finite; a program needn't handle non-finite values.
Results may differ from the reference program's by a relative error of at most 0.0001.
Values sent between devices are 32-bit elements; how exact they have to be, the bound alone decides.
A program may use at most 128 MiB of HBM per device.

```python
import jax
import jax.numpy as jnp
from jax import lax

LEAF = 256
RANK = 128
COLS = 128
LEVELS = 9
POINTS = 131072


def draw_leaf_inverse(key, part):
    key = jax.random.fold_in(key, 11)
    key_diag, key_off = jax.random.split(key)
    leaves = POINTS // LEAF
    spread = 0.25 / LEAF ** 0.5
    diag_vals = jax.random.uniform(key_diag, (leaves, LEAF), jnp.float32, 0.7, 1.5)
    noise = jnp.clip(jax.random.normal(key_off, (leaves, LEAF, LEAF), jnp.float32), -6.0, 6.0)
    noise = (noise + jnp.swapaxes(noise, 1, 2)) * (spread / 2.0 ** 0.5)
    blocks = noise + jnp.eye(LEAF, dtype=jnp.float32)[None] * diag_vals[:, None, :]
    return blocks.reshape(POINTS, LEAF)


def draw_bases(key, part):
    key = jax.random.fold_in(key, 23)
    scales = jnp.sqrt(0.15 / (LEAF * 2.0 ** jnp.arange(LEVELS, dtype=jnp.float32)))
    values = jnp.clip(jax.random.normal(key, (LEVELS, POINTS, RANK), jnp.float32), -5.0, 5.0)
    return values * scales[:, None, None]


def levels(own_key, shape, shards, low, top_value):
    gain = 1.0
    for axis_at, parts in shards:
        heights = jax.random.uniform(jax.random.fold_in(jax.random.fold_in(own_key, 6), axis_at), (parts,), jnp.float32, low / len(shards), top_value / len(shards))
        gain = gain * jnp.repeat(jnp.exp(heights), shape[axis_at] // parts).reshape((-1,) + (1,) * (len(shape) - 1 - axis_at))
    return gain


def centred(own_key, shape, deviation, most, cuts=(), held_as=jnp.bfloat16):
    drawn = deviation * jax.random.normal(own_key, shape, jnp.float32)
    if cuts:
        drawn = drawn * levels(own_key, shape, cuts, -0.22, 0.18)
    return jnp.clip(drawn, -most, most).astype(held_as)


def setup_inputs(seed: int = 0) -> dict:
    key_list = jax.random.split(jax.random.key(seed), 4)
    return {
        "right_side": centred(key_list[0], (POINTS, COLS), 1.0, 6.0, ((0, 512),), jnp.float32),
        "leaf_inverse": draw_leaf_inverse(jax.random.fold_in(key_list[3], 71), 0),
        "bases": draw_bases(jax.random.fold_in(key_list[3], 71), 0),
    }


HIGH = lax.Precision.HIGHEST

def core_solve(own_half, sibling_half):
    basis_rank = own_half.shape[0]
    g_own = own_half[:, -basis_rank:]
    s_own = own_half[:, :-basis_rank]
    g_other = sibling_half[:, -basis_rank:]
    s_other = sibling_half[:, :-basis_rank]
    system = jnp.eye(basis_rank, dtype=jnp.float32) - jnp.dot(g_other.astype(jnp.float32), g_own.astype(jnp.float32), precision=HIGH, preferred_element_type=jnp.float32)
    right_part = s_other - jnp.dot(g_other.astype(jnp.float32), s_own.astype(jnp.float32), precision=HIGH, preferred_element_type=jnp.float32)
    normal = jnp.dot(system.T.astype(jnp.float32), system.astype(jnp.float32), precision=HIGH, preferred_element_type=jnp.float32)
    factor = jnp.linalg.cholesky(normal)
    return jax.scipy.linalg.cho_solve((factor, True), jnp.dot(system.T.astype(jnp.float32), right_part.astype(jnp.float32), precision=HIGH, preferred_element_type=jnp.float32))

def reference(right_side, leaf_inverse, bases):
    leaves = POINTS // LEAF
    stacked = jnp.concatenate([right_side] + [bases[index_level] for index_level in reversed(range(LEVELS))], axis=1)
    inverses = leaf_inverse.reshape(leaves, LEAF, LEAF)
    current = jnp.einsum('npq,nqc->npc', inverses, stacked.reshape(leaves, LEAF, -1), precision=HIGH)
    current = current.reshape(POINTS, -1)
    for tree_level in range(1, LEVELS + 1):
        active_cols = current.shape[1]
        half_rows = LEAF * 2 ** (tree_level - 1)
        groups = POINTS // (2 * half_rows)
        active = current.reshape(groups, 2, half_rows, active_cols)
        level_basis = bases[tree_level - 1].reshape(groups, 2, half_rows, RANK)
        projected = jnp.einsum('ghpr,ghpc->ghrc', level_basis, active, precision=HIGH)
        sibling_half = projected[:, ::-1]
        weights = jax.vmap(jax.vmap(core_solve))(projected, sibling_half)
        updated = active[..., :active_cols - RANK] - jnp.einsum('ghpr,ghrc->ghpc', active[..., active_cols - RANK:], weights, precision=HIGH)
        current = updated.reshape(POINTS, active_cols - RANK)
    return current
```

```python
import functools

import jax
import jax.numpy as jnp
from jax import lax
from jax.experimental import pallas as pl
from jax.experimental.pallas import tpu as pltpu
from jax.sharding import PartitionSpec as P

F32 = jnp.float32
RANK = 128
PARTNERS = ((0,), (1,), (1, 2), (3,), (4,), (5,), (5, 6), (7,), (7, 8))
RING = ((1,), (2,), (1, 2))
CORE = (0,)


def dot(a, b):
    return jnp.dot(a, b, precision=lax.Precision.HIGH, preferred_element_type=F32)


def dot6(a, b):
    return jnp.dot(a, b, precision=lax.Precision.HIGHEST, preferred_element_type=F32)


def bit(index, b):
    return lax.rem(lax.div(index, 2**b), 2)


def flipped(index, bits):
    for b in bits:
        index = index + (1 - 2 * bit(index, b)) * 2**b
    return index


def chebyshev_heights(count, at):
    heights = [at]
    for _ in range(count):
        heights.append(2 * heights[-1] ** 2 - 1)
    return heights


def inverse(g_own, g_other, midway):
    rows = lax.broadcasted_iota(jnp.int32, (RANK, RANK), 0)
    cols = lax.broadcasted_iota(jnp.int32, (RANK, RANK), 1)
    eye = jnp.where(rows == cols, 1.0, 0.0).astype(F32)
    system = eye - dot6(g_other, g_own)
    system_t = eye - dot6(g_own, g_other)
    normal = dot6(system_t, system)
    heights = chebyshev_heights(5, 1.25)
    poly = 1.25 * eye - normal
    result = system_t
    scale = 1.0 / heights[5]
    for step in range(5):
        if step == 2:
            midway()
        result = dot6(eye + poly * (1.0 / heights[step]), result)
        scale = scale * 2 * heights[step]
        if step < 4:
            poly = 2.0 * dot6(poly, poly) - eye
    return result * scale


def kernel(levels, n_sems, right_ref, inv_ref, bases_ref, out_ref, work, *scratch):
    def width(level):
        return (levels + 2 - level) * RANK

    def slice_rows(level):
        return RANK // min(2 ** (level - 1), 8)

    scratch = list(scratch)
    own, other, total = {}, {}, {}
    mine, theirs, coef, turned = {}, {}, {}, {}
    for level in range(1, levels + 1):
        own[level] = scratch.pop(0)
        other[level] = scratch.pop(0)
        if level < levels:
            coef[level] = scratch.pop(0)
            turned[level] = scratch.pop(0)
            total[level] = scratch.pop(0)
        for row in range(level + 1, levels + 1):
            mine[level, row] = scratch.pop(0)
            theirs[level, row] = scratch.pop(0)
    send_sem, recv_sem = scratch

    me = lax.axis_index("leaf")
    core = bit(me, 0)
    low_split = lax.rem(bit(me, 1) + bit(me, 2), 2)
    high_split = bit(me, 2)
    offsets = {1: 0, 2: 64 * core, 3: 64 * core + 32 * low_split}
    after = 64 * core + 32 * low_split + 16 * high_split

    def offset(level):
        return offsets.get(level, after)

    def partner_part(level):
        return {1: 64 * (1 - core), 2: 32 * (1 - low_split), 3: 16 * (1 - high_split)}.get(level, 0)

    def own_part(level):
        return {1: 64 * core, 2: 32 * low_split, 3: 16 * high_split}.get(level, 0)

    def rows_at(start, size):
        return pl.ds(start if isinstance(start, int) else pl.multiple_of(start, 16), size)

    count = [0]
    pending = []

    def send(src, dst, bits):
        k = count[0]
        count[0] += 1
        copy = pltpu.make_async_remote_copy(
            src_ref=src,
            dst_ref=dst,
            send_sem=send_sem.at[k],
            recv_sem=recv_sem.at[k],
            device_id=(flipped(me, bits),),
            device_id_type=pl.DeviceIdType.MESH,
        )
        copy.start()
        pending.append(copy)
        return copy

    partners = set(PARTNERS[:levels])
    if levels >= 3:
        partners |= set(RING)
    partners = sorted(partners | {CORE})
    barrier = pltpu.get_barrier_semaphore()
    for bits in partners:
        pl.semaphore_signal(
            barrier, inc=1, device_id=(flipped(me, bits),), device_id_type=pl.DeviceIdType.MESH
        )

    work[:, :RANK] = dot(inv_ref[...], right_ref[...])
    for level in range(levels, 0, -1):
        at = (levels + 1 - level) * RANK
        work[:, at : at + RANK] = dot(inv_ref[...], bases_ref[level - 1])
    own[1][...] = dot(bases_ref[0].T, work[...])
    for row in range(2, levels + 1):
        mine[1, row][...] = dot(bases_ref[row - 1].T, work[:, : width(row)])

    pl.semaphore_wait(barrier, len(partners))

    def start_gather(ref, level, cols):
        here = ref.at[rows_at(offset(level), slice_rows(level)), cols]
        ring = {2: (), 3: ((1,),)}.get(level, RING)
        return [send(here, here, bits) for bits in ring]

    def forward(ref, cols, copies):
        for copy in copies:
            copy.wait_recv()
        here = ref.at[rows_at(64 * core, 64), cols]
        return send(here, here, CORE)

    for level in range(1, levels + 1):
        bits = PARTNERS[level - 1]
        rest = width(level) - RANK
        wide, narrow = slice(rest, rest + RANK), slice(0, rest)
        size, next_size = slice_rows(level), slice_rows(level + 1)
        last = level == levels
        a_ref, b_ref = own[level], other[level]
        settled = list(pending)
        pending.clear()

        here = rows_at(offset(level), size)
        got_g = send(a_ref.at[here, wide], b_ref.at[here, wide], bits)
        got_rest = send(a_ref.at[here, narrow], b_ref.at[here, narrow], bits)
        got_rows = {}
        for row in range(level + 1, levels + 1):
            src = mine[level, row]
            if row > level + 1 and next_size < size:
                src = src.at[rows_at(partner_part(level), next_size)]
            got_rows[row] = send(src, theirs[level, row], bits)

        if level > 1:
            old = width(level)
            work[:, :old] = work[:, :old] - dot(work[:, old : old + RANK], coef[level - 1][:RANK])
        for copy in settled:
            copy.wait_send()
        if not last:
            for row in range(level + 1, levels + 1):
                at = (levels + 1 - row) * RANK
                turned[level][at - RANK : at, :RANK] = a_ref[:, at : at + RANK].T

        def add_next():
            got_rows[level + 1].wait_recv()
            total[level][here] = mine[level, level + 1][...] + theirs[level, level + 1][...]

        got_g.wait_recv()
        if level == 1:
            got_rest.wait_recv()
            if not last:
                add_next()
            x = inverse(a_ref[:, wide], b_ref[:, wide], lambda: None)
        else:
            ring_g = start_gather(b_ref, level, wide)
            got_rest.wait_recv()
            ring_rest = start_gather(b_ref, level, narrow)
            if not last:
                add_next()
                ring_total = start_gather(total[level], level, slice(None))
            core_g = forward(b_ref, wide, ring_g)
            core_rest = forward(b_ref, narrow, ring_rest)
            core_total = []
            core_g.wait_recv()

            def midway():
                if not last:
                    core_total.append(forward(total[level], slice(None), ring_total))

            x = inverse(a_ref[:, wide], b_ref[:, wide], midway)
            core_rest.wait_recv()

        a_rest, b_rest = a_ref[:, narrow], b_ref[:, narrow]
        coef_own = dot(x, b_rest - dot(b_ref[:, wide], a_rest))
        if last:
            out_ref[...] = work[:, :RANK] - dot(work[:, RANK : 2 * RANK], coef_own)
            break
        coef[level][:RANK] = coef_own
        coef[level][RANK:] = dot(x.T, a_rest - dot(a_ref[:, wide], b_rest))
        for row in range(level + 1, levels + 1):
            at = (levels + 1 - row) * RANK
            turned[level][at - RANK : at, RANK:] = b_ref[:, at : at + RANK].T
        if level > 1:
            core_total[0].wait_recv()
        own[level + 1][...] = total[level][...] - dot(
            turned[level][rest - 2 * RANK : rest - RANK, :], coef[level][...]
        )
        later = list(range(level + 2, levels + 1))
        if later:
            left = []
            for row in later:
                at = (levels - row) * RANK
                left.append(turned[level][rows_at(at + offset(level + 1), next_size), :])
            change = dot(jnp.concatenate(left, axis=0), coef[level][:, : width(level + 2)])
            for i, row in enumerate(later):
                got_rows[row].wait_recv()
                kept = mine[level, row][rows_at(own_part(level), next_size), :]
                mine[level + 1, row][...] = (
                    kept
                    + theirs[level, row][...]
                    - change[i * next_size : (i + 1) * next_size, : width(row)]
                )

    for copy in pending:
        copy.wait_send()
    assert count[0] == n_sems, count[0]


def n_copies(levels):
    total = 0
    for level in range(1, levels + 1):
        total += 2 + levels - level
        if level > 1:
            parts = 2 if level == levels else 3
            total += parts * ({2: 0, 3: 1}.get(level, 3) + 1)
    return total


def shards(right_side, leaf_inverse, bases):
    levels = bases.shape[0]
    n_sems = n_copies(levels)

    def width(level):
        return (levels + 2 - level) * RANK

    def slice_rows(level):
        return RANK // min(2 ** (level - 1), 8)

    def buffer(rows, cols):
        return pltpu.VMEM((rows, cols), F32)

    scratch = [buffer(right_side.shape[0], width(1))]
    for level in range(1, levels + 1):
        scratch += [buffer(RANK, width(level))] * 2
        if level < levels:
            scratch.append(buffer(2 * RANK, width(level + 1)))
            scratch.append(buffer(width(level + 1) - RANK, 2 * RANK))
            scratch.append(buffer(RANK, width(level + 1)))
        for row in range(level + 1, levels + 1):
            size = slice_rows(level)
            scratch.append(buffer(size, width(row)))
            scratch.append(buffer(size if row == level + 1 else slice_rows(level + 1), width(row)))
    scratch += [pltpu.SemaphoreType.DMA((n_sems,))] * 2
    vmem = pl.BlockSpec(memory_space=pltpu.VMEM)
    return pl.pallas_call(
        functools.partial(kernel, levels, n_sems),
        out_shape=jax.ShapeDtypeStruct(right_side.shape, F32),
        in_specs=[vmem] * 3,
        out_specs=vmem,
        scratch_shapes=scratch,
        compiler_params=pltpu.CompilerParams(
            collective_id=0, has_side_effects=True, vmem_limit_bytes=48 * 2**20
        ),
        name="tree_solve",
    )(right_side, leaf_inverse, bases)


def solution(mesh):
    return jax.shard_map(
        shards,
        mesh=mesh,
        in_specs=(P("leaf", None), P("leaf", None), P(None, "leaf", None)),
        out_specs=P("leaf", None),
        check_vma=False,
    )
```

```python
import functools

import jax
import jax.numpy as jnp
from jax import lax
from jax.experimental import pallas as pl
from jax.experimental.pallas import tpu as pltpu
from jax.sharding import PartitionSpec as P

F32 = jnp.float32
RANK = 128
PARTNERS = ((0,), (1,), (1, 2), (3,), (4,), (5,), (5, 6), (7,), (7, 8))
RING = ((1,), (2,), (1, 2))
CORE = (0,)
AROUND = ((1,), (1, 2), CORE, (0, 1), (0, 1, 2), (2,), (0, 2))
WIDE = 8
STRAIGHT = 6


def dot(a, b):
    return jnp.dot(a, b, precision=lax.Precision.HIGH, preferred_element_type=F32)


def dot6(a, b):
    return jnp.dot(a, b, precision=lax.Precision.HIGHEST, preferred_element_type=F32)


def bit(index, b):
    return lax.rem(lax.div(index, 2**b), 2)


def flipped(index, bits):
    for b in bits:
        index = index + (1 - 2 * bit(index, b)) * 2**b
    return index


def chebyshev_heights(count, at):
    heights = [at]
    for _ in range(count):
        heights.append(2 * heights[-1] ** 2 - 1)
    return heights


def inverse(g_own, g_other, hook):
    rows = lax.broadcasted_iota(jnp.int32, (RANK, RANK), 0)
    cols = lax.broadcasted_iota(jnp.int32, (RANK, RANK), 1)
    eye = jnp.where(rows == cols, 1.0, 0.0).astype(F32)
    system = eye - dot6(g_other, g_own)
    system_t = eye - dot6(g_own, g_other)
    normal = dot6(system_t, system)
    heights = chebyshev_heights(5, 1.25)
    poly = 1.25 * eye - normal
    result = system_t
    scale = 1.0 / heights[5]
    for step in range(5):
        hook(step)
        result = dot6(eye + poly * (1.0 / heights[step]), result)
        scale = scale * 2 * heights[step]
        if step < 4:
            poly = 2.0 * dot6(poly, poly) - eye
    return result * scale


def slice_rows(level):
    if level >= WIDE:
        return 64
    return RANK // min(2 ** (level - 1), 8)


def row_rows(level):
    return 64 if level == 3 else slice_rows(level)


def ring_of(level):
    if level == 2 or level >= WIDE:
        return ()
    return ((1,),) if level == 3 else RING


def around_of(level):
    if level == 2 or level >= WIDE:
        return (CORE,)
    return ((1,), CORE, (0, 1)) if level == 3 else AROUND


def straight(level, first):
    return level >= STRAIGHT or first or ring_of(level) == ()


def n_copies(levels):
    total = 0
    for level in range(1, levels + 1):
        total += 2 + levels - level
        if level > 1:
            for part in range(2 if level == levels else 3):
                if level == 3 and part < 2:
                    total += 1
                elif straight(level, part == 0):
                    total += len(around_of(level))
                else:
                    total += len(ring_of(level)) + 1
            if level == WIDE - 1:
                total += (levels - level - 1) * len(ring_of(level))
    return total


def kernel(levels, n_sems, right_hbm, inv_hbm, bases_hbm, out_ref, work, *scratch):
    def width(level):
        return (levels + 2 - level) * RANK

    scratch = list(scratch)
    right_ref, inv_ref, bases_ref = scratch[:3]
    del scratch[:3]
    own, other, total = {}, {}, {}
    mine, theirs, coef, turned, summed = {}, {}, {}, {}, {}
    for level in range(1, levels + 1):
        own[level] = scratch.pop(0)
        other[level] = scratch.pop(0)
        if level < levels:
            coef[level] = scratch.pop(0)
            turned[level] = scratch.pop(0)
            total[level] = scratch.pop(0)
        for row in range(level + 1, levels + 1):
            mine[level, row] = scratch.pop(0)
            theirs[level, row] = scratch.pop(0)
            if level == WIDE - 1 and row > level + 1:
                summed[row] = scratch.pop(0)
    load_sem, send_sem, recv_sem = scratch

    loads = []
    for k, (src, dst) in enumerate(
        (
            (inv_hbm, inv_ref),
            (bases_hbm.at[0], bases_ref.at[0]),
            (right_hbm, right_ref),
            (bases_hbm.at[pl.ds(1, levels - 1)], bases_ref.at[pl.ds(1, levels - 1)]),
        )
    ):
        loads.append(pltpu.make_async_copy(src, dst, load_sem.at[k]))
        loads[-1].start()

    me = lax.axis_index("leaf")
    core = bit(me, 0)
    low_split = lax.rem(bit(me, 1) + bit(me, 2), 2)
    high_split = bit(me, 2)
    half = 64 * core
    quarter = half + 32 * low_split
    eighth = quarter + 16 * high_split

    def offset(level):
        if level == 1:
            return 0
        if level == 2 or level >= WIDE:
            return half
        return quarter if level == 3 else eighth

    def partner_part(level):
        return {1: 64 * (1 - core), 2: 32 * (1 - low_split), 3: 16 * (1 - high_split)}[level]

    def own_part(level):
        return {1: 64 * core, 2: 32 * low_split, 3: 16 * high_split}[level]

    def rows_at(start, size):
        return pl.ds(start if isinstance(start, int) else pl.multiple_of(start, 16), size)

    count = [0]
    pending = []

    def send(src, dst, bits):
        nonlocal pending
        k = count[0]
        count[0] += 1
        copy = pltpu.make_async_remote_copy(
            src_ref=src,
            dst_ref=dst,
            send_sem=send_sem.at[k],
            recv_sem=recv_sem.at[k],
            device_id=(flipped(me, bits),),
            device_id_type=pl.DeviceIdType.MESH,
        )
        copy.start()
        pending.append(copy)
        return copy

    partners = set(PARTNERS[:levels]) | {CORE}
    for level in range(2, levels + 1):
        partners |= set(around_of(level))
    partners = sorted(partners)
    barrier = pltpu.get_barrier_semaphore()
    for bits in partners:
        pl.semaphore_signal(
            barrier, inc=1, device_id=(flipped(me, bits),), device_id_type=pl.DeviceIdType.MESH
        )

    def leaf_work(level):
        at = (levels + 1 - level) * RANK
        work[:, at : at + RANK] = dot(inv_ref[...], bases_ref[level - 1])

    loads[0].wait()
    loads[1].wait()
    leaf_work(1)
    top = width(1) - RANK
    own[1][:, top:] = dot(bases_ref[0].T, work[:, top:])

    pl.semaphore_wait(barrier, len(partners))

    def gather(ref, level, cols, first):
        if level == 3 and ref is other[3]:
            here = ref.at[rows_at(half, 64), cols]
            return (ref, cols, [send(here, here, CORE)], True)
        here = ref.at[rows_at(offset(level), slice_rows(level)), cols]
        whole = straight(level, first)
        copies = [send(here, here, bits) for bits in (around_of if whole else ring_of)(level)]
        return (ref, cols, copies, whole)

    def forward(started):
        ref, cols, copies, whole = started
        if whole:
            return started
        for copy in copies:
            copy.wait_recv()
        here = ref.at[rows_at(half, 64), cols]
        return (ref, cols, [send(here, here, CORE)], True)

    def finish(started):
        for copy in started[2]:
            copy.wait_recv()

    got_rows = {}

    def send_row(level, row):
        size, next_size = slice_rows(level), slice_rows(level + 1)
        src = mine[level, row]
        if row > level + 1 and next_size < size:
            src = src.at[rows_at(partner_part(level), next_size)]
        got_rows[level, row] = send(src, theirs[level, row], PARTNERS[level - 1])

    def update_rows(level, rows):
        if not rows:
            return
        before, size = level - 1, slice_rows(level)
        left = []
        for row in rows:
            at = (levels - row) * RANK
            left.append(turned[before][rows_at(at + offset(level), size), :])
        left = left[0] if len(left) == 1 else jnp.concatenate(left, axis=0)
        change = dot(left, coef[before][:, : width(rows[0])])
        for i, row in enumerate(rows):
            if row in summed and level == WIDE:
                base = summed[row][rows_at(half, 64), :]
            else:
                got_rows[before, row].wait_recv()
                base = mine[before, row]
                if size < slice_rows(before):
                    base = base.at[rows_at(own_part(before), size)]
                base = base[...] + theirs[before, row][...]
            mine[level, row][...] = base - change[i * size : (i + 1) * size, : width(row)]
            send_row(level, row)

    def leaf_rows(rows):
        for row in rows:
            mine[1, row][...] = dot(bases_ref[row - 1].T, work[:, : width(row)])
            send_row(1, row)

    sent = []
    for level in range(1, levels + 1):
        bits = PARTNERS[level - 1]
        rest = width(level) - RANK
        wide, narrow = slice(rest, rest + RANK), slice(0, rest)
        last = level == levels
        a_ref, b_ref = own[level], other[level]
        sent.append(pending)
        pending = []
        later = list(range(level + 2, levels + 1))
        following = [] if last else [level + 1]
        here = rows_at(offset(level), slice_rows(level))
        mid = rows_at(half if level == 3 else offset(level), row_rows(level))

        def send_part(cols):
            return send(a_ref.at[mid, cols], b_ref.at[mid, cols], bits)

        def turn(ref, at_col):
            for row in range(level + 1, levels + 1):
                at = (levels + 1 - row) * RANK
                turned[level][at - RANK : at, at_col : at_col + RANK] = ref[:, at : at + RANK].T

        def settle():
            old = width(level)
            work[:, :old] = work[:, :old] - dot(work[:, old : old + RANK], coef[level - 1][:RANK])
            turn(a_ref, 0)
            if level > 2:
                for copy in sent[level - 2]:
                    copy.wait_send()

        def add_next():
            got_rows[level, level + 1].wait_recv()
            total[level][here] = mine[level, level + 1][...] + theirs[level, level + 1][...]

        def gather_next():
            if last:
                return []
            add_next()
            return [gather(total[level], level, slice(None), False)]

        got_g = send_part(wide)
        if level == 1:
            for copy in loads[2:]:
                copy.wait()
            work[:, :RANK] = dot(inv_ref[...], right_ref[...])
            for row in range(levels, 1, -1):
                leaf_work(row)
            a_ref[:, narrow] = dot(bases_ref[0].T, work[:, narrow])
            got_rest = send_part(narrow)
            leaf_rows(following)
            got_g.wait_recv()
            x = inverse(a_ref[:, wide], b_ref[:, wide], lambda step: leaf_rows(later[step : step + 1]))
            leaf_rows(later[5:])
            turn(a_ref, 0)
            got_rest.wait_recv()
        elif level <= 3:
            if level == 2:
                got_rest = send_part(narrow)
            update_rows(level, following)
            if level == 3:
                got_rest = send_part(narrow)
            settle()
            if level == 2:
                update_rows(level, later)
            got_g.wait_recv()
            finish(gather(b_ref, level, wide, True))
            x = inverse(a_ref[:, wide], b_ref[:, wide], lambda step: None)
            if level == 2:
                got_rest.wait_recv()
                all_rest = gather(b_ref, level, narrow, False)
                all_total = gather_next()
            else:
                all_total = gather_next()
                got_rest.wait_recv()
                all_rest = gather(b_ref, level, narrow, False)
                all_total = [forward(part) for part in all_total]
                update_rows(level, later)
            finish(all_rest)
        else:
            got_rest = send_part(narrow)
            if level > 4:
                update_rows(level, following)
            settle()
            got_g.wait_recv()
            all_g = gather(b_ref, level, wide, True)
            got_rest.wait_recv()
            held = [gather(b_ref, level, narrow, False)]
            if level == 4:
                update_rows(level, following)
            update_rows(level, later)
            all_total = [] if level >= WIDE else gather_next()
            finish(all_g)

            def hook(step):
                if step == 2:
                    held[0] = forward(held[0])
                if step == 3 and level >= WIDE:
                    all_total.extend(gather_next())

            x = inverse(a_ref[:, wide], b_ref[:, wide], hook)
            all_total = [forward(part) for part in all_total]
            if level == WIDE - 1:
                spread = []
                for row in later:
                    got_rows[level, row].wait_recv()
                    summed[row][here] = mine[level, row][...] + theirs[level, row][...]
                    part = summed[row].at[here]
                    spread += [send(part, part, ring) for ring in ring_of(level)]
            finish(held[0])

        a_rest, b_rest = a_ref[:, narrow], b_ref[:, narrow]
        coef_own = dot(x, b_rest - dot(b_ref[:, wide], a_rest))
        if last:
            out_ref[...] = work[:, :RANK] - dot(work[:, RANK : 2 * RANK], coef_own)
            break
        coef[level][:RANK] = coef_own
        coef[level][RANK:] = dot(x.T, a_rest - dot(a_ref[:, wide], b_rest))
        turn(b_ref, RANK)
        if level == 1:
            add_next()
        for part in all_total if level > 1 else ():
            finish(part)
        own[level + 1][...] = total[level][...] - dot(
            turned[level][rest - 2 * RANK : rest - RANK, :], coef[level][...]
        )
        if level == WIDE - 1:
            for copy in spread:
                copy.wait_recv()

    for copy in sum(sent[-1:], []) + pending:
        copy.wait_send()
    assert count[0] == n_sems, count[0]


def shards(right_side, leaf_inverse, bases):
    levels = bases.shape[0]
    n_sems = n_copies(levels)

    def width(level):
        return (levels + 2 - level) * RANK

    def buffer(*shape):
        return pltpu.VMEM(shape, F32)

    scratch = [buffer(right_side.shape[0], width(1))]
    scratch += [buffer(*right_side.shape), buffer(*leaf_inverse.shape), buffer(*bases.shape)]
    for level in range(1, levels + 1):
        scratch += [buffer(RANK, width(level))] * 2
        if level < levels:
            scratch.append(buffer(2 * RANK, width(level + 1)))
            scratch.append(buffer(width(level + 1) - RANK, 2 * RANK))
            scratch.append(buffer(RANK, width(level + 1)))
        for row in range(level + 1, levels + 1):
            size, next_size = slice_rows(level), slice_rows(level + 1)
            scratch.append(buffer(size, width(row)))
            scratch.append(buffer(size if row == level + 1 else min(size, next_size), width(row)))
            if level == WIDE - 1 and row > level + 1:
                scratch.append(buffer(RANK, width(row)))
    scratch.append(pltpu.SemaphoreType.DMA((4,)))
    scratch += [pltpu.SemaphoreType.DMA((n_sems,))] * 2
    return pl.pallas_call(
        functools.partial(kernel, levels, n_sems),
        out_shape=jax.ShapeDtypeStruct(right_side.shape, F32),
        in_specs=[pl.BlockSpec(memory_space=pl.ANY)] * 3,
        out_specs=pl.BlockSpec(memory_space=pltpu.VMEM),
        scratch_shapes=scratch,
        compiler_params=pltpu.CompilerParams(
            collective_id=0, has_side_effects=True, vmem_limit_bytes=56 * 2**20
        ),
        name="tree_solve",
    )(right_side, leaf_inverse, bases)


def solution(mesh):
    return jax.shard_map(
        shards,
        mesh=mesh,
        in_specs=(P("leaf", None), P("leaf", None), P(None, "leaf", None)),
        out_specs=P("leaf", None),
        check_vma=False,
    )
```

```python
import functools

import jax
import jax.numpy as jnp
from jax import lax
from jax.experimental import pallas as pl
from jax.experimental.pallas import tpu as pltpu
from jax.sharding import PartitionSpec as P

F32 = jnp.float32
RANK = 128
PARTNERS = ((0,), (1,), (1, 2), (3,), (4,), (5,), (5, 6), (7,), (7, 8))
RING = ((1,), (2,), (1, 2))
CORE = (0,)
AROUND = ((1,), (1, 2), CORE, (0, 1), (0, 1, 2), (2,), (0, 2))
WIDE = 8
HALVED = (3, 4)
STRAIGHT = 6


def dot(a, b):
    return jnp.dot(a, b, precision=lax.Precision.HIGH, preferred_element_type=F32)


def bit(index, b):
    return lax.rem(lax.div(index, 2**b), 2)


def flipped(index, bits):
    for b in bits:
        index = index + (1 - 2 * bit(index, b)) * 2**b
    return index


def chebyshev_heights(count, at):
    heights = [at]
    for _ in range(count):
        heights.append(2 * heights[-1] ** 2 - 1)
    return heights


def inverse(g_own, g_other, hook):
    rows = lax.broadcasted_iota(jnp.int32, (RANK, RANK), 0)
    cols = lax.broadcasted_iota(jnp.int32, (RANK, RANK), 1)
    eye = jnp.where(rows == cols, 1.0, 0.0).astype(F32)
    q, q_t = dot(g_other, g_own), dot(g_own, g_other)
    normal = eye - q - q_t + dot(q_t, q)
    heights = chebyshev_heights(5, 1.25)
    scale = 1.0 / heights[5]
    for height in heights[:5]:
        scale = scale * 2 * height
    poly = eye - 0.8 * normal
    result = (eye - q_t) * scale
    for step in range(5):
        hook(step)
        if step == 4:
            return result + jnp.dot(poly, result, preferred_element_type=F32)
        result = result + dot(poly, result)
        part = 1.0 / heights[step + 1]
        poly = (1.0 + part) * dot(poly, poly) - part * eye


def slice_rows(level):
    if level >= WIDE:
        return 64
    return RANK // min(2 ** (level - 1), 8)


def ring_of(level):
    if level == 2 or level >= WIDE:
        return ()
    return ((1,),) if level == 3 else RING


def around_of(level):
    if level == 2 or level >= WIDE:
        return (CORE,)
    return ((1,), CORE, (0, 1)) if level == 3 else AROUND


def straight(level, first):
    return level >= STRAIGHT or first or ring_of(level) == ()


def n_copies(levels):
    total = 0
    for level in range(1, levels + 1):
        total += 2 + levels - level
        if level == 2:
            total += max(levels - 3, 0)
        if level > 1:
            for part in range(2 if level == levels else 3):
                if level in HALVED and part == 0:
                    total += 1
                elif level == 3 and part == 2:
                    total += len(RING) + 1
                elif straight(level, part == 0):
                    total += len(around_of(level))
                else:
                    total += len(ring_of(level)) + 1
            if level == WIDE - 1:
                total += (levels - level - 1) * len(ring_of(level))
    return total


def kernel(levels, n_sems, right_hbm, inv_hbm, bases_hbm, out_ref, work, *scratch):
    def width(level):
        return (levels + 2 - level) * RANK

    scratch = list(scratch)
    right_ref, inv_ref, bases_ref = scratch[:3]
    del scratch[:3]
    both, total = {}, {}
    mine, theirs, coef, turned, summed = {}, {}, {}, {}, {}
    early, relayed = {}, {}
    for level in range(1, levels + 1):
        both[level] = scratch.pop(0)
        if level < levels:
            coef[level] = scratch.pop(0)
            turned[level] = scratch.pop(0)
            total[level] = scratch.pop(0)
        for row in range(level + 1, levels + 1):
            mine[level, row] = scratch.pop(0)
            theirs[level, row] = scratch.pop(0)
            if level == 2 and row > 3:
                early[row], relayed[row] = scratch.pop(0), scratch.pop(0)
            if level == WIDE - 1 and row > level + 1:
                summed[row] = scratch.pop(0)
    core_ref, load_sem, send_sem, recv_sem = scratch

    loads = []
    for k, (src, dst) in enumerate(
        (
            (inv_hbm, inv_ref),
            (bases_hbm.at[pl.ds(0, 2)], bases_ref.at[pl.ds(0, 2)]),
            (right_hbm, right_ref),
            (bases_hbm.at[pl.ds(2, levels - 2)], bases_ref.at[pl.ds(2, levels - 2)]),
        )
    ):
        loads.append(pltpu.make_async_copy(src, dst, load_sem.at[k]))
        loads[-1].start()

    me = lax.axis_index("leaf")
    core = bit(me, 0)
    low_split = lax.rem(bit(me, 1) + bit(me, 2), 2)
    high_split = bit(me, 2)
    half = 64 * core
    quarter = half + 32 * low_split
    eighth = quarter + 16 * high_split

    def offset(level):
        if level == 1:
            return 0
        if level == 2 or level >= WIDE:
            return half
        return quarter if level == 3 else eighth

    def partner_part(level):
        return {1: 64 * (1 - core), 2: 32 * (1 - low_split), 3: 16 * (1 - high_split)}[level]

    def own_part(level):
        return {1: 64 * core, 2: 32 * low_split, 3: 16 * high_split}[level]

    def rows_at(start, size):
        return pl.ds(start if isinstance(start, int) else pl.multiple_of(start, 16), size)

    count = [0]
    pending = []

    def send(src, dst, bits):
        nonlocal pending
        k = count[0]
        count[0] += 1
        copy = pltpu.make_async_remote_copy(
            src_ref=src,
            dst_ref=dst,
            send_sem=send_sem.at[k],
            recv_sem=recv_sem.at[k],
            device_id=(flipped(me, bits),),
            device_id_type=pl.DeviceIdType.MESH,
        )
        copy.start()
        pending.append(copy)
        return copy

    partners = set(PARTNERS[:levels]) | {CORE}
    for level in range(2, levels + 1):
        partners |= set(around_of(level))
    partners = sorted(partners)
    barrier = pltpu.get_barrier_semaphore()
    for bits in partners:
        pl.semaphore_signal(
            barrier, inc=1, device_id=(flipped(me, bits),), device_id_type=pl.DeviceIdType.MESH
        )

    def leaf_work(level):
        at = (levels + 1 - level) * RANK
        work[:, at : at + RANK] = dot(inv_ref[...], bases_ref[level - 1])

    loads[0].wait()
    loads[1].wait()
    leaf_work(1)
    leaf_work(2)
    top = width(1) - 2 * RANK
    both[1][RANK:, top:] = dot(bases_ref[0].T, work[:, top:])

    pl.semaphore_wait(barrier, len(partners))

    def gather(ref, level, cols, first):
        ahead = level == 3 and ref is not both[3]
        whole = straight(level, first)
        here = rows_at(eighth, 16) if ahead else rows_at(offset(level), slice_rows(level))
        if first and level in HALVED:
            here = rows_at(half, 64)
            return (ref, cols, [send(ref.at[here, cols], ref.at[here, cols], CORE)], True)
        here = ref.at[here, cols]
        ring = RING if ahead else ring_of(level)
        copies = [send(here, here, bits) for bits in (around_of(level) if whole else ring)]
        return (ref, cols, copies, whole)

    def forward(started):
        ref, cols, copies, whole = started
        if whole:
            return started
        for copy in copies:
            copy.wait_recv()
        here = ref.at[rows_at(half, 64), cols]
        return (ref, cols, [send(here, here, CORE)], True)

    def finish(started):
        for copy in started[2]:
            copy.wait_recv()

    got_rows, got_early = {}, {}
    spread = []

    def send_row(level, row):
        size, next_size = slice_rows(level), slice_rows(level + 1)
        src = mine[level, row]
        if level == 2 and row > 3:
            part = rows_at(32 * (1 - low_split) + 16 * (1 - high_split), 16)
            got_early[row] = send(src.at[part], early[row], PARTNERS[2])
            return
        if (row > level + 1 or level == 3) and next_size < size:
            src = src.at[rows_at(partner_part(level), next_size)]
        got_rows[level, row] = send(src, theirs[level, row], PARTNERS[level - 1])

    def relay(rows):
        for row in rows:
            got_early[row].wait_recv()
            part = rows_at(32 * (1 - low_split) + 16 * high_split, 16)
            relayed[row][...] = mine[2, row][part, :] + early[row][...]
            got_rows[2, row] = send(relayed[row], theirs[2, row], PARTNERS[1])

    def update_rows(level, rows):
        if not rows:
            return
        before, size = level - 1, slice_rows(level)
        left = []
        for row in rows:
            at = (levels - row) * RANK
            left.append(turned[before][rows_at(at + offset(level), size), :])
        left = left[0] if len(left) == 1 else jnp.concatenate(left, axis=0)
        change = dot(left, coef[before][:, : width(rows[0])])
        for i, row in enumerate(rows):
            if row in summed and level == WIDE:
                while spread:
                    spread.pop().wait_recv()
                base = summed[row][rows_at(half, 64), :]
            else:
                base = mine[before, row]
                if size < slice_rows(before):
                    base = base.at[rows_at(own_part(before), size)]
                base = base[...]
                for node in {2: (), 3: (2, 3)}.get(before, (before,)):
                    got_rows[node, row].wait_recv()
                    base = base + theirs[node, row][...]
            mine[level, row][...] = base - change[i * size : (i + 1) * size, : width(row)]
            send_row(level, row)

    def leaf_rows(rows):
        for row in rows:
            mine[1, row][...] = dot(bases_ref[row - 1].T, work[:, : width(row)])
            send_row(1, row)

    sent = []
    for level in range(1, levels + 1):
        bits = PARTNERS[level - 1]
        last = level == levels
        g_at = width(level) - RANK
        rest = g_at if last or level in HALVED else g_at - RANK
        wide, narrow, g_cols = slice(rest, None), slice(0, rest), slice(g_at, None)
        ab = both[level]
        sent.append(pending)
        pending = []
        later = list(range(level + 2, levels + 1))
        following = [] if last else [level + 1]
        here = rows_at(offset(level), slice_rows(level))

        def send_part(cols):
            size, start = slice_rows(level), offset(level)
            if level in HALVED and cols is wide:
                size, start = 64, half
            return send(
                ab.at[rows_at(start + RANK, size), cols], ab.at[rows_at(start, size), cols], bits
            )

        def turn(node, rows, first, to):
            for row in rows:
                at = (levels + 1 - row) * RANK
                block = both[node][first : first + RANK, at : at + RANK]
                turned[node][at - RANK : at, to : to + RANK] = block.T

        def settle_coef():
            before = level - 1
            turn(before, range(level + 1, levels + 1), 0, RANK)
            coef[before][...] = dot(core_ref[...], both[before][:, : width(level)])

        def settle():
            old = width(level)
            work[:, :old] = work[:, :old] - dot(work[:, old : old + RANK], coef[level - 1][:RANK])
            turn(level, range(level + 1, levels + 1), RANK, 0)
            if level > 2:
                for copy in sent[level - 2]:
                    copy.wait_send()

        def add_next():
            got_rows[level, level + 1].wait_recv()
            if level == 3:
                got_rows[2, 4].wait_recv()
                kept = mine[3, 4][rows_at(own_part(3), 16), :] + theirs[2, 4][...]
                total[3][rows_at(eighth, 16)] = kept + theirs[3, 4][...]
                return
            total[level][here] = mine[level, level + 1][...] + theirs[level, level + 1][...]

        def gather_next():
            if last:
                return []
            add_next()
            return [gather(total[level], level, slice(None), False)]

        def solve(hooks):
            return inverse(
                ab[RANK:, g_cols], ab[:RANK, g_cols], lambda step: hooks.get(step, lambda: None)()
            )

        got_wide = send_part(wide)
        if level == 1:
            for copy in loads[2:]:
                copy.wait()
            work[:, :RANK] = dot(inv_ref[...], right_ref[...])
            for row in range(levels, 2, -1):
                leaf_work(row)
            ab[RANK:, narrow] = dot(bases_ref[0].T, work[:, narrow])
            got_rest = send_part(narrow)
            leaf_rows(following)
            got_wide.wait_recv()
            x = solve({2: lambda: leaf_rows(later[:1])})
            turn(level, range(2, levels + 1), RANK, 0)
        elif level == 2:
            got_rest = send_part(narrow)
            settle_coef()
            update_rows(level, following)
            got_wide.wait_recv()
            all_wide = gather(ab, level, wide, True)
            leaf_rows(later)
            settle()
            update_rows(level, later)
            finish(all_wide)
            x = solve({})
        else:
            got_rest = send_part(narrow)
            settle_coef()
            update_rows(level, following)
            got_wide.wait_recv()
            all_wide = gather(ab, level, wide, True)
            got_rest.wait_recv()
            held = [gather(ab, level, narrow, False)]
            settle()
            if level > 3:
                update_rows(level, later)
            all_total = [] if level >= WIDE else gather_next()
            if level == 3:
                update_rows(level, later)
            finish(all_wide)

            def pass_on():
                held[0] = forward(held[0])
                if last:
                    finish(held[0])

            hooks = {4 if level == 3 else 2: pass_on}
            if level >= WIDE:
                hooks[3] = lambda: all_total.extend(gather_next())
            x = solve(hooks)

        if last:
            right = ab[:RANK, narrow] - dot(ab[:RANK, g_cols], ab[RANK:, narrow])
            out_ref[...] = work[:, :RANK] - dot(work[:, RANK : 2 * RANK], dot(x, right))
            break

        x_t = x.T
        core_ref[:RANK, :RANK] = x
        core_ref[RANK:, RANK:] = x_t
        core_ref[:RANK, RANK:] = -dot(x, ab[:RANK, g_cols])
        core_ref[RANK:, :RANK] = -dot(x_t, ab[RANK:, g_cols])

        def left_side():
            turn(level, [level + 1], 0, RANK)
            return dot(turned[level][g_at - 2 * RANK : g_at - RANK, :], core_ref[...])

        if level not in HALVED:
            left = left_side()
        if level == 1:
            got_rest.wait_recv()
        elif level == 2:
            got_rest.wait_recv()
            all_rest = gather(ab, level, narrow, False)
            relay(later)
            all_total = gather_next()
            finish(all_rest)
        else:
            all_total = [forward(part) for part in all_total]
            if level == WIDE - 1:
                for row in later:
                    got_rows[level, row].wait_recv()
                    summed[row][here] = mine[level, row][...] + theirs[level, row][...]
                    part = summed[row].at[here]
                    spread += [send(part, part, ring) for ring in ring_of(level)]
            finish(held[0])
        if level in HALVED:
            left = left_side()
        change = dot(left, ab[:, : width(level + 1)])
        if level == 1:
            add_next()
        else:
            for part in all_total:
                finish(part)
        both[level + 1][RANK:, :] = total[level][...] - change

    for copy in sum(sent[-1:], []) + pending:
        copy.wait_send()
    assert count[0] == n_sems, count[0]


def shards(right_side, leaf_inverse, bases):
    levels = bases.shape[0]
    n_sems = n_copies(levels)

    def width(level):
        return (levels + 2 - level) * RANK

    def buffer(*shape):
        return pltpu.VMEM(shape, F32)

    scratch = [buffer(right_side.shape[0], width(1))]
    scratch += [buffer(*right_side.shape), buffer(*leaf_inverse.shape), buffer(*bases.shape)]
    for level in range(1, levels + 1):
        scratch.append(buffer(2 * RANK, width(level)))
        if level < levels:
            scratch.append(buffer(2 * RANK, width(level + 1)))
            scratch.append(buffer(width(level + 1) - RANK, 2 * RANK))
            scratch.append(buffer(RANK, width(level + 1)))
        for row in range(level + 1, levels + 1):
            size, next_size = slice_rows(level), slice_rows(level + 1)
            scratch.append(buffer(size, width(row)))
            full = row == level + 1 and level != 3
            size = 16 if level in (2, 3) and row > 3 else size if full else min(size, next_size)
            scratch.append(buffer(size, width(row)))
            if level == 2 and row > 3:
                scratch += [buffer(size, width(row))] * 2
            if level == WIDE - 1 and row > level + 1:
                scratch.append(buffer(RANK, width(row)))
    scratch.append(buffer(2 * RANK, 2 * RANK))
    scratch.append(pltpu.SemaphoreType.DMA((4,)))
    scratch += [pltpu.SemaphoreType.DMA((n_sems,))] * 2
    return pl.pallas_call(
        functools.partial(kernel, levels, n_sems),
        out_shape=jax.ShapeDtypeStruct(right_side.shape, F32),
        in_specs=[pl.BlockSpec(memory_space=pl.ANY)] * 3,
        out_specs=pl.BlockSpec(memory_space=pltpu.VMEM),
        scratch_shapes=scratch,
        compiler_params=pltpu.CompilerParams(
            collective_id=0, has_side_effects=True, vmem_limit_bytes=56 * 2**20
        ),
        name="tree_solve",
    )(right_side, leaf_inverse, bases)


def solution(mesh):
    return jax.shard_map(
        shards,
        mesh=mesh,
        in_specs=(P("leaf", None), P("leaf", None), P(None, "leaf", None)),
        out_specs=P("leaf", None),
        check_vma=False,
    )
```

```python
import functools

import jax
import jax.numpy as jnp
from jax import lax
from jax.experimental import pallas as pl
from jax.experimental.pallas import tpu as pltpu
from jax.sharding import PartitionSpec as P

F32 = jnp.float32
RANK = 128
PARTNERS = ((0,), (1,), (1, 2), (3,), (4,), (5,), (5, 6), (7,), (7, 8))
RING = ((2,), (1, 2), (1,))
CORE = (0,)
AROUND = ((0, 2), (2,), (0, 1, 2), (1, 2), (0, 1), (1,), CORE)
WIDE = 8
HALVED = (3, 4)
STRAIGHT = 8


def dot(a, b):
    return jnp.dot(a, b, precision=lax.Precision.HIGH, preferred_element_type=F32)


def bit(index, b):
    return lax.rem(lax.div(index, 2**b), 2)


def flipped(index, bits):
    for b in bits:
        index = index + (1 - 2 * bit(index, b)) * 2**b
    return index


def chebyshev_heights(count, at):
    heights = [at]
    for _ in range(count):
        heights.append(2 * heights[-1] ** 2 - 1)
    return heights


def inverses(pairs, hook):
    rows = lax.broadcasted_iota(jnp.int32, (RANK, RANK), 0)
    cols = lax.broadcasted_iota(jnp.int32, (RANK, RANK), 1)
    eye = jnp.where(rows == cols, 1.0, 0.0).astype(F32)
    heights = chebyshev_heights(5, 1.25)
    scale = 1.0 / heights[5]
    for height in heights[:5]:
        scale = scale * 2 * height
    qs = [(dot(g_other, g_own), dot(g_own, g_other)) for g_own, g_other in pairs]
    polys = [eye - 0.8 * (eye - q - q_t + dot(q_t, q)) for q, q_t in qs]
    results = [(eye - q_t) * scale for q, q_t in qs]
    for step in range(4):
        hook(step)
        results = [result + dot(poly, result) for poly, result in zip(polys, results)]
        part = 1.0 / heights[step + 1]
        polys = [(1.0 + part) * dot(poly, poly) - part * eye for poly in polys]
    hook(4)
    return [
        result + jnp.dot(poly, result, preferred_element_type=F32)
        for poly, result in zip(polys, results)
    ]


def slice_rows(level):
    if level >= WIDE:
        return 64
    return RANK // min(2 ** (level - 1), 8)


def ring_of(level):
    if level == 2 or level >= WIDE:
        return ()
    return ((1,),) if level == 3 else RING


def around_of(level):
    if level == 2 or level >= WIDE:
        return (CORE,)
    return ((1,), CORE, (0, 1)) if level == 3 else AROUND


def straight(level, first):
    return level >= STRAIGHT or first or ring_of(level) == ()


def n_copies(levels):
    total = 0
    for level in range(1, levels + 1):
        if level == WIDE:
            return total + 17
        total += 2 + levels - level
        if level == 2:
            total += max(levels - 3, 0)
        if level > 1:
            for part in range(2 if level == levels else 3):
                if level in HALVED and part == 0:
                    total += 1
                elif level == 3 and part == 2:
                    total += len(RING) + 1
                elif straight(level, part == 0):
                    total += len(around_of(level))
                else:
                    total += len(ring_of(level)) + 1
            if level == WIDE - 1:
                total += (levels - level - 1) * len(ring_of(level))
    return total


def kernel(levels, n_sems, right_hbm, inv_hbm, bases_hbm, out_ref, work, *scratch):
    def width(level):
        return (levels + 2 - level) * RANK

    scratch = list(scratch)
    right_ref, inv_ref, bases_ref = scratch[:3]
    del scratch[:3]
    both, total = {}, {}
    mine, theirs, coef, turned, summed = {}, {}, {}, {}, {}
    early, relayed = {}, {}
    for level in range(1, levels + 1):
        both[level] = scratch.pop(0)
        if level < levels:
            coef[level] = scratch.pop(0)
            turned[level] = scratch.pop(0)
            total[level] = scratch.pop(0)
        for row in range(level + 1, levels + 1):
            mine[level, row] = scratch.pop(0)
            theirs[level, row] = scratch.pop(0)
            if level == 2 and row > 3:
                early[row], relayed[row] = scratch.pop(0), scratch.pop(0)
            if level == WIDE - 1 and row > level + 1:
                summed[row] = scratch.pop(0)
    core_ref, core_far, both_far, turned_far, total_far, nine_far, load_sem, send_sem, recv_sem = scratch

    loads = []
    for k, (src, dst) in enumerate(
        (
            (inv_hbm, inv_ref),
            (bases_hbm.at[pl.ds(0, 2)], bases_ref.at[pl.ds(0, 2)]),
            (right_hbm, right_ref),
            (bases_hbm.at[pl.ds(2, levels - 2)], bases_ref.at[pl.ds(2, levels - 2)]),
        )
    ):
        loads.append(pltpu.make_async_copy(src, dst, load_sem.at[k]))
        loads[-1].start()

    me = lax.axis_index("leaf")
    core = bit(me, 0)
    low_split = lax.rem(bit(me, 1) + bit(me, 2), 2)
    high_split = bit(me, 2)
    half = 64 * core
    quarter = half + 32 * low_split
    eighth = quarter + 16 * high_split

    def offset(level):
        if level == 1:
            return 0
        if level == 2 or level >= WIDE:
            return half
        return quarter if level == 3 else eighth

    def partner_part(level):
        return {1: 64 * (1 - core), 2: 32 * (1 - low_split), 3: 16 * (1 - high_split)}[level]

    def own_part(level):
        return {1: 64 * core, 2: 32 * low_split, 3: 16 * high_split}[level]

    def rows_at(start, size):
        return pl.ds(start if isinstance(start, int) else pl.multiple_of(start, 16), size)

    count = [0]
    pending = []

    def send(src, dst, bits):
        nonlocal pending
        k = count[0]
        count[0] += 1
        copy = pltpu.make_async_remote_copy(
            src_ref=src,
            dst_ref=dst,
            send_sem=send_sem.at[k],
            recv_sem=recv_sem.at[k],
            device_id=(flipped(me, bits),),
            device_id_type=pl.DeviceIdType.MESH,
        )
        copy.start()
        pending.append(copy)
        return copy

    partners = set(PARTNERS[:levels]) | {CORE}
    for level in range(2, levels + 1):
        partners |= set(around_of(level))
    quarters = ()
    if levels > WIDE:
        near, far = PARTNERS[WIDE - 1 : WIDE + 1]
        quarters = (near, far, tuple(sorted(set(near) ^ set(far))))
    partners = sorted(partners | set(quarters))
    barrier = pltpu.get_barrier_semaphore()
    for bits in partners:
        pl.semaphore_signal(
            barrier, inc=1, device_id=(flipped(me, bits),), device_id_type=pl.DeviceIdType.MESH
        )

    def leaf_work(level):
        at = (levels + 1 - level) * RANK
        work[:, at : at + RANK] = dot(inv_ref[...], bases_ref[level - 1])

    loads[0].wait()
    loads[1].wait()
    leaf_work(1)
    leaf_work(2)
    top = width(1) - 2 * RANK
    both[1][RANK:, top:] = dot(bases_ref[0].T, work[:, top:])

    pl.semaphore_wait(barrier, len(partners))

    def gather(ref, level, cols, first):
        ahead = level == 3 and ref is not both[3]
        whole = straight(level, first)
        here = rows_at(eighth, 16) if ahead else rows_at(offset(level), slice_rows(level))
        if first and level in HALVED:
            here = rows_at(half, 64)
            return (ref, cols, [send(ref.at[here, cols], ref.at[here, cols], CORE)], True)
        here = ref.at[here, cols]
        ring = RING if ahead else ring_of(level)
        copies = [send(here, here, bits) for bits in (around_of(level) if whole else ring)]
        return (ref, cols, copies, whole)

    def forward(started):
        ref, cols, copies, whole = started
        if whole:
            return started
        for copy in copies:
            copy.wait_recv()
        here = ref.at[rows_at(half, 64), cols]
        return (ref, cols, [send(here, here, CORE)], True)

    def finish(started):
        for copy in started[2]:
            copy.wait_recv()

    got_rows, got_early = {}, {}
    spread, got_nine = [], []

    def send_row(level, row):
        size, next_size = slice_rows(level), slice_rows(level + 1)
        src = mine[level, row]
        if level == WIDE:
            for way, dst in zip(quarters, (theirs[level, row], nine_far.at[0], nine_far.at[1])):
                got_nine.append(send(src, dst, way))
            return
        if level == 2 and row > 3:
            part = rows_at(32 * (1 - low_split) + 16 * (1 - high_split), 16)
            got_early[row] = send(src.at[part], early[row], PARTNERS[2])
            return
        if (row > level + 1 or level == 3) and next_size < size:
            src = src.at[rows_at(partner_part(level), next_size)]
        got_rows[level, row] = send(src, theirs[level, row], PARTNERS[level - 1])

    def relay(rows):
        for row in rows:
            got_early[row].wait_recv()
            part = rows_at(32 * (1 - low_split) + 16 * high_split, 16)
            relayed[row][...] = mine[2, row][part, :] + early[row][...]
            got_rows[2, row] = send(relayed[row], theirs[2, row], PARTNERS[1])

    def update_rows(level, rows):
        if not rows:
            return
        before, size = level - 1, slice_rows(level)
        left = []
        for row in rows:
            at = (levels - row) * RANK
            left.append(turned[before][rows_at(at + offset(level), size), :])
        left = left[0] if len(left) == 1 else jnp.concatenate(left, axis=0)
        change = dot(left, coef[before][:, : width(rows[0])])
        for i, row in enumerate(rows):
            if row in summed and level == WIDE:
                while spread:
                    spread.pop().wait_recv()
                base = summed[row][rows_at(half, 64), :]
            else:
                base = mine[before, row]
                if size < slice_rows(before):
                    base = base.at[rows_at(own_part(before), size)]
                base = base[...]
                for node in {2: (), 3: (2, 3)}.get(before, (before,)):
                    got_rows[node, row].wait_recv()
                    base = base + theirs[node, row][...]
            mine[level, row][...] = base - change[i * size : (i + 1) * size, : width(row)]
            send_row(level, row)

    def leaf_rows(rows):
        for row in rows:
            mine[1, row][...] = dot(bases_ref[row - 1].T, work[:, : width(row)])
            send_row(1, row)

    sent = []
    for level in range(1, levels + 1):
        bits = PARTNERS[level - 1]
        last = level == levels
        g_at = width(level) - RANK
        rest = g_at if last or level in HALVED or level == WIDE else g_at - RANK
        wide, narrow, g_cols = slice(rest, None), slice(0, rest), slice(g_at, None)
        ab = both[level]
        sent.append(pending)
        pending = []
        later = list(range(level + 2, levels + 1))
        following = [] if last else [level + 1]
        here = rows_at(offset(level), slice_rows(level))

        def send_part(cols):
            size, start = slice_rows(level), offset(level)
            if level in HALVED and cols is wide:
                size, start = 64, half
            return send(
                ab.at[rows_at(start + RANK, size), cols], ab.at[rows_at(start, size), cols], bits
            )

        def turn(node, rows, first, to):
            for row in rows:
                at = (levels + 1 - row) * RANK
                block = both[node][first : first + RANK, at : at + RANK]
                turned[node][at - RANK : at, to : to + RANK] = block.T

        def settle_coef():
            before = level - 1
            turn(before, range(level + 1, levels + 1), 0, RANK)
            coef[before][...] = dot(core_ref[...], both[before][:, : width(level)])

        def settle():
            old = width(level)
            work[:, :old] = work[:, :old] - dot(work[:, old : old + RANK], coef[level - 1][:RANK])
            turn(level, range(level + 1, levels + 1), RANK, 0)
            if level > 2:
                for copy in sent[level - 2]:
                    copy.wait_send()

        def add_next():
            got_rows[level, level + 1].wait_recv()
            if level == 3:
                got_rows[2, 4].wait_recv()
                kept = mine[3, 4][rows_at(own_part(3), 16), :] + theirs[2, 4][...]
                total[3][rows_at(eighth, 16)] = kept + theirs[3, 4][...]
                return
            total[level][here] = mine[level, level + 1][...] + theirs[level, level + 1][...]

        def gather_next():
            if last:
                return []
            add_next()
            return [gather(total[level], level, slice(None), False)]

        def solve(hooks):
            pairs = [(ab[RANK:, g_cols], ab[:RANK, g_cols])]
            return inverses(pairs, lambda step: hooks.get(step, lambda: None)())[0]

        def core_of(x, ref, into):
            x_t = x.T
            into[:RANK, :RANK] = x
            into[RANK:, RANK:] = x_t
            into[:RANK, RANK:] = -dot(x, ref[:RANK, g_cols])
            into[RANK:, :RANK] = -dot(x_t, ref[RANK:, g_cols])

        if level == WIDE:
            def send_all(cols):
                src = ab.at[rows_at(half + RANK, 64), cols]
                return [
                    send(src, ab.at[rows_at(half, 64), cols], quarters[0]),
                    send(src, both_far.at[rows_at(half + RANK, 64), cols], quarters[1]),
                    send(src, both_far.at[rows_at(half, 64), cols], quarters[2]),
                ]

            def share(copies, cols):
                shared = []
                spots = ((ab, half), (both_far, half + RANK), (both_far, half))
                for copy, (ref, start) in zip(copies, spots):
                    copy.wait_recv()
                    part = ref.at[rows_at(start, 64), cols]
                    shared.append(send(part, part, CORE))
                return shared

            got_wide = send_all(wide)
            got_rest = send_all(narrow)
            settle_coef()
            update_rows(level, following)
            core_wide = share(got_wide, wide)
            settle()
            core_rest = share(got_rest, narrow)
            for copy in core_wide:
                copy.wait_recv()
            core_nine = []

            def add_nine(step):
                if step != 4:
                    return
                for copy in got_nine:
                    copy.wait_recv()
                part = rows_at(half, 64)
                total[level][part] = mine[level, levels][...] + theirs[level, levels][...]
                total_far[part] = nine_far[0] + nine_far[1]
                for ref in (total[level], total_far):
                    core_nine.append(send(ref.at[part], ref.at[part], CORE))

            x, x_far = inverses(
                [
                    (ab[RANK:, g_cols], ab[:RANK, g_cols]),
                    (both_far[RANK:, g_cols], both_far[:RANK, g_cols]),
                ],
                add_nine,
            )
            core_of(x, ab, core_ref)
            core_of(x_far, both_far, core_far)
            for copy in core_rest:
                copy.wait_recv()
            turn(level, [levels], 0, RANK)
            turned_far[:, :RANK] = both_far[RANK:, RANK : 2 * RANK].T
            turned_far[:, RANK:] = both_far[:RANK, RANK : 2 * RANK].T
            left = dot(turned[level][...], core_ref[...])
            left_far = dot(turned_far[...], core_far[...])
            change = dot(left, ab[:, : 2 * RANK])
            change_far = dot(left_far, both_far[:, : 2 * RANK])
            for copy in core_nine:
                copy.wait_recv()
            nine = total[level][...] - change
            nine_other = total_far[...] - change_far
            g_own, g_other = nine[:, RANK:], nine_other[:, RANK:]
            (x,) = inverses([(g_own, g_other)], lambda step: None)
            cols = 2 * RANK
            coef_own = dot(core_ref[:RANK, :], ab[:, :cols])
            after = work[:, :cols] - dot(work[:, cols : cols + RANK], coef_own)
            right = nine_other[:, :RANK] - dot(g_other, nine[:, :RANK])
            out_ref[...] = after[:, :RANK] - dot(after[:, RANK:], dot(x, right))
            break

        got_wide = send_part(wide)
        if level == 1:
            for copy in loads[2:]:
                copy.wait()
            work[:, :RANK] = dot(inv_ref[...], right_ref[...])
            for row in range(levels, 2, -1):
                leaf_work(row)
            ab[RANK:, narrow] = dot(bases_ref[0].T, work[:, narrow])
            got_rest = send_part(narrow)
            leaf_rows(following)
            got_wide.wait_recv()
            x = solve({2: lambda: leaf_rows(later[:1])})
            turn(level, range(2, levels + 1), RANK, 0)
        elif level == 2:
            got_rest = send_part(narrow)
            settle_coef()
            update_rows(level, following)
            got_wide.wait_recv()
            all_wide = gather(ab, level, wide, True)
            leaf_rows(later)
            settle()
            update_rows(level, later)
            finish(all_wide)
            x = solve({})
        else:
            got_rest = send_part(narrow)
            settle_coef()
            update_rows(level, following)
            got_wide.wait_recv()
            all_wide = gather(ab, level, wide, True)
            got_rest.wait_recv()
            held = [gather(ab, level, narrow, False)]
            if level > 3:
                update_rows(level, later)
            if level >= 6:
                settle()
            all_total = gather_next()
            if level == 3:
                update_rows(level, later)
            if level < 6:
                settle()
            finish(all_wide)

            def pass_on():
                held[0] = forward(held[0])

            x = solve({} if level == 4 else {4 if level == 3 else 2: pass_on})
            if level == 5:
                all_total = [forward(part) for part in all_total]

        if last:
            right = ab[:RANK, narrow] - dot(ab[:RANK, g_cols], ab[RANK:, narrow])
            out_ref[...] = work[:, :RANK] - dot(work[:, RANK : 2 * RANK], dot(x, right))
            break

        core_of(x, ab, core_ref)
        if level == 4:
            pass_on()

        def left_side():
            turn(level, [level + 1], 0, RANK)
            return dot(turned[level][g_at - 2 * RANK : g_at - RANK, :], core_ref[...])

        if level not in HALVED:
            left = left_side()
        if level == 1:
            got_rest.wait_recv()
        elif level == 2:
            got_rest.wait_recv()
            all_rest = gather(ab, level, narrow, False)
            relay(later)
            all_total = gather_next()
            finish(all_rest)
        else:
            all_total = [forward(part) for part in all_total]
            if level == WIDE - 1:
                for row in later:
                    got_rows[level, row].wait_recv()
                    summed[row][here] = mine[level, row][...] + theirs[level, row][...]
                    part = summed[row].at[here]
                    spread += [send(part, part, ring) for ring in ring_of(level)]
            finish(held[0])
        if level in HALVED:
            left = left_side()
        change = dot(left, ab[:, : width(level + 1)])
        if level == 1:
            add_next()
        else:
            for part in all_total:
                finish(part)
        both[level + 1][RANK:, :] = total[level][...] - change

    for copy in sum(sent[-1:], []) + pending:
        copy.wait_send()
    assert count[0] == n_sems, count[0]


def shards(right_side, leaf_inverse, bases):
    levels = bases.shape[0]
    n_sems = n_copies(levels)

    def width(level):
        return (levels + 2 - level) * RANK

    def buffer(*shape):
        return pltpu.VMEM(shape, F32)

    scratch = [buffer(right_side.shape[0], width(1))]
    scratch += [buffer(*right_side.shape), buffer(*leaf_inverse.shape), buffer(*bases.shape)]
    for level in range(1, levels + 1):
        scratch.append(buffer(2 * RANK, width(level)))
        if level < levels:
            scratch.append(buffer(2 * RANK, width(level + 1)))
            scratch.append(buffer(width(level + 1) - RANK, 2 * RANK))
            scratch.append(buffer(RANK, width(level + 1)))
        for row in range(level + 1, levels + 1):
            size, next_size = slice_rows(level), slice_rows(level + 1)
            scratch.append(buffer(size, width(row)))
            full = row == level + 1 and level != 3
            size = 16 if level in (2, 3) and row > 3 else size if full else min(size, next_size)
            scratch.append(buffer(size, width(row)))
            if level == 2 and row > 3:
                scratch += [buffer(size, width(row))] * 2
            if level == WIDE - 1 and row > level + 1:
                scratch.append(buffer(RANK, width(row)))
    scratch += [buffer(2 * RANK, 2 * RANK)] * 2
    scratch += [buffer(2 * RANK, 3 * RANK), buffer(RANK, 2 * RANK), buffer(RANK, 2 * RANK)]
    scratch.append(buffer(2, 64, 2 * RANK))
    scratch.append(pltpu.SemaphoreType.DMA((4,)))
    scratch += [pltpu.SemaphoreType.DMA((n_sems,))] * 2
    return pl.pallas_call(
        functools.partial(kernel, levels, n_sems),
        out_shape=jax.ShapeDtypeStruct(right_side.shape, F32),
        in_specs=[pl.BlockSpec(memory_space=pl.ANY)] * 3,
        out_specs=pl.BlockSpec(memory_space=pltpu.VMEM),
        scratch_shapes=scratch,
        compiler_params=pltpu.CompilerParams(
            collective_id=0, has_side_effects=True, vmem_limit_bytes=56 * 2**20
        ),
        name="tree_solve",
    )(right_side, leaf_inverse, bases)


def solution(mesh):
    return jax.shard_map(
        shards,
        mesh=mesh,
        in_specs=(P("leaf", None), P("leaf", None), P(None, "leaf", None)),
        out_specs=P("leaf", None),
        check_vma=False,
    )
```

```python
import functools

import jax
import jax.numpy as jnp
from jax import lax
from jax.experimental import pallas as pl
from jax.experimental.pallas import tpu as pltpu
from jax.sharding import PartitionSpec as P

F32 = jnp.float32
RANK = 128
PARTNERS = ((0,), (1,), (1, 2), (3,), (4,), (5,), (5, 6), (7,), (7, 8))
RING = ((2,), (1, 2), (1,))
CORE = (0,)
AROUND = ((0, 2), (2,), (0, 1, 2), (1, 2), (0, 1), (1,), CORE)
WIDE = 8
HALVED = (3, 4)
STRAIGHT = 8


def dot(a, b):
    return jnp.dot(a, b, precision=lax.Precision.HIGH, preferred_element_type=F32)


def bit(index, b):
    return lax.rem(lax.div(index, 2**b), 2)


def flipped(index, bits):
    for b in bits:
        index = index + (1 - 2 * bit(index, b)) * 2**b
    return index


def chebyshev_heights(count, at):
    heights = [at]
    for _ in range(count):
        heights.append(2 * heights[-1] ** 2 - 1)
    return heights


def inverses(pairs, hook):
    rows = lax.broadcasted_iota(jnp.int32, (RANK, RANK), 0)
    cols = lax.broadcasted_iota(jnp.int32, (RANK, RANK), 1)
    eye = jnp.where(rows == cols, 1.0, 0.0).astype(F32)
    heights = chebyshev_heights(5, 1.25)
    scale = 1.0 / heights[5]
    for height in heights[:5]:
        scale = scale * 2 * height
    qs = [(dot(g_other, g_own), dot(g_own, g_other)) for g_own, g_other in pairs]
    polys = [eye - 0.8 * (eye - q - q_t + dot(q_t, q)) for q, q_t in qs]
    results = [(eye - q_t) * scale for q, q_t in qs]
    for step in range(4):
        hook(step)
        results = [result + dot(poly, result) for poly, result in zip(polys, results)]
        part = 1.0 / heights[step + 1]
        polys = [(1.0 + part) * dot(poly, poly) - part * eye for poly in polys]
    hook(4)
    return [
        result + jnp.dot(poly, result, preferred_element_type=F32)
        for poly, result in zip(polys, results)
    ]


def slice_rows(level):
    if level >= WIDE:
        return 64
    return RANK // min(2 ** (level - 1), 8)


def ring_of(level):
    if level == 2 or level >= WIDE:
        return ()
    return ((1,),) if level == 3 else RING


def around_of(level):
    if level == 2 or level >= WIDE:
        return (CORE,)
    return ((1,), CORE, (0, 1)) if level == 3 else AROUND


def straight(level, first):
    return level >= STRAIGHT or first or ring_of(level) == ()


def n_copies(levels):
    total = 0
    for level in range(1, levels + 1):
        if level == WIDE:
            return total + 17
        total += 2 + levels - level
        if level == 2:
            total += max(levels - 3, 0)
        if level > 1:
            for part in range(2 if level == levels else 3):
                if level in HALVED and part == 0:
                    total += 1
                elif level == 3 and part == 2:
                    total += len(RING) + 1
                elif straight(level, part == 0):
                    total += len(around_of(level))
                else:
                    total += len(ring_of(level)) + 1
            if level == WIDE - 1:
                total += (levels - level - 1) * len(ring_of(level))
    return total


def kernel(levels, n_sems, right_hbm, inv_hbm, bases_hbm, out_ref, work, *scratch):
    def width(level):
        return (levels + 2 - level) * RANK

    scratch = list(scratch)
    right_ref, inv_ref, bases_ref = scratch[:3]
    del scratch[:3]
    both, total = {}, {}
    mine, theirs, coef, turned, summed = {}, {}, {}, {}, {}
    early, relayed = {}, {}
    for level in range(1, levels + 1):
        both[level] = scratch.pop(0)
        if level < levels:
            coef[level] = scratch.pop(0)
            turned[level] = scratch.pop(0)
            total[level] = scratch.pop(0)
        for row in range(level + 1, levels + 1):
            mine[level, row] = scratch.pop(0)
            theirs[level, row] = scratch.pop(0)
            if level == 2 and row > 3:
                early[row], relayed[row] = scratch.pop(0), scratch.pop(0)
            if level == WIDE - 1 and row > level + 1:
                summed[row] = scratch.pop(0)
    core_ref, core_far, both_far, turned_far, total_far, nine_far, load_sem, send_sem, recv_sem = scratch

    loads = []
    for k, (src, dst) in enumerate(
        (
            (inv_hbm, inv_ref),
            (bases_hbm.at[pl.ds(0, 2)], bases_ref.at[pl.ds(0, 2)]),
            (right_hbm, right_ref),
            (bases_hbm.at[pl.ds(2, levels - 2)], bases_ref.at[pl.ds(2, levels - 2)]),
        )
    ):
        loads.append(pltpu.make_async_copy(src, dst, load_sem.at[k]))
        loads[-1].start()

    me = lax.axis_index("leaf")
    core = bit(me, 0)
    low_split = lax.rem(bit(me, 1) + bit(me, 2), 2)
    high_split = bit(me, 2)
    half = 64 * core
    quarter = half + 32 * low_split
    eighth = quarter + 16 * high_split

    def offset(level):
        if level == 1:
            return 0
        if level == 2 or level >= WIDE:
            return half
        return quarter if level == 3 else eighth

    def partner_part(level):
        return {1: 64 * (1 - core), 2: 32 * (1 - low_split), 3: 16 * (1 - high_split)}[level]

    def own_part(level):
        return {1: 64 * core, 2: 32 * low_split, 3: 16 * high_split}[level]

    def rows_at(start, size):
        return pl.ds(start if isinstance(start, int) else pl.multiple_of(start, 16), size)

    count = [0]
    pending = []

    def send(src, dst, bits):
        nonlocal pending
        k = count[0]
        count[0] += 1
        copy = pltpu.make_async_remote_copy(
            src_ref=src,
            dst_ref=dst,
            send_sem=send_sem.at[k],
            recv_sem=recv_sem.at[k],
            device_id=(flipped(me, bits),),
            device_id_type=pl.DeviceIdType.MESH,
        )
        copy.start()
        pending.append(copy)
        return copy

    partners = set(PARTNERS[:levels]) | {CORE}
    for level in range(2, levels + 1):
        partners |= set(around_of(level))
    quarters = ()
    if levels > WIDE:
        near, far = PARTNERS[WIDE - 1 : WIDE + 1]
        quarters = (near, far, tuple(sorted(set(near) ^ set(far))))
    partners = sorted(partners | set(quarters))
    barrier = pltpu.get_barrier_semaphore()
    for bits in partners:
        pl.semaphore_signal(
            barrier, inc=1, device_id=(flipped(me, bits),), device_id_type=pl.DeviceIdType.MESH
        )

    def leaf_work(level):
        at = (levels + 1 - level) * RANK
        work[:, at : at + RANK] = dot(inv_ref[...], bases_ref[level - 1])

    loads[0].wait()
    loads[1].wait()
    leaf_work(1)
    leaf_work(2)
    top = width(1) - 2 * RANK
    both[1][RANK:, top:] = dot(bases_ref[0].T, work[:, top:])

    pl.semaphore_wait(barrier, len(partners))

    def gather(ref, level, cols, first):
        ahead = level == 3 and ref is not both[3]
        whole = straight(level, first)
        here = rows_at(eighth, 16) if ahead else rows_at(offset(level), slice_rows(level))
        if first and level in HALVED:
            here = rows_at(half, 64)
            return (ref, cols, [send(ref.at[here, cols], ref.at[here, cols], CORE)], True)
        here = ref.at[here, cols]
        ring = RING if ahead else ring_of(level)
        copies = [send(here, here, bits) for bits in (around_of(level) if whole else ring)]
        return (ref, cols, copies, whole)

    def forward(started):
        ref, cols, copies, whole = started
        if whole:
            return started
        for copy in copies:
            copy.wait_recv()
        here = ref.at[rows_at(half, 64), cols]
        return (ref, cols, [send(here, here, CORE)], True)

    def finish(started):
        for copy in started[2]:
            copy.wait_recv()

    got_rows, got_early = {}, {}
    spread, got_nine = [], []

    def send_row(level, row):
        size, next_size = slice_rows(level), slice_rows(level + 1)
        src = mine[level, row]
        if level == WIDE:
            for way, dst in zip(quarters, (theirs[level, row], nine_far.at[0], nine_far.at[1])):
                got_nine.append(send(src, dst, way))
            return
        if level == 2 and row > 3:
            part = rows_at(32 * (1 - low_split) + 16 * (1 - high_split), 16)
            got_early[row] = send(src.at[part], early[row], PARTNERS[2])
            return
        if (row > level + 1 or level == 3) and next_size < size:
            src = src.at[rows_at(partner_part(level), next_size)]
        got_rows[level, row] = send(src, theirs[level, row], PARTNERS[level - 1])

    def relay(rows):
        for row in rows:
            got_early[row].wait_recv()
            part = rows_at(32 * (1 - low_split) + 16 * high_split, 16)
            relayed[row][...] = mine[2, row][part, :] + early[row][...]
            got_rows[2, row] = send(relayed[row], theirs[2, row], PARTNERS[1])

    def update_rows(level, rows):
        if not rows:
            return
        before, size = level - 1, slice_rows(level)
        left = []
        for row in rows:
            at = (levels - row) * RANK
            left.append(turned[before][rows_at(at + offset(level), size), :])
        left = left[0] if len(left) == 1 else jnp.concatenate(left, axis=0)
        change = dot(left, coef[before][:, : width(rows[0])])
        for i, row in enumerate(rows):
            if row in summed and level == WIDE:
                while spread:
                    spread.pop().wait_recv()
                base = summed[row][rows_at(half, 64), :]
            else:
                base = mine[before, row]
                if size < slice_rows(before):
                    base = base.at[rows_at(own_part(before), size)]
                base = base[...]
                for node in {2: (), 3: (2, 3)}.get(before, (before,)):
                    got_rows[node, row].wait_recv()
                    base = base + theirs[node, row][...]
            mine[level, row][...] = base - change[i * size : (i + 1) * size, : width(row)]
            send_row(level, row)

    def leaf_rows(rows):
        for row in rows:
            mine[1, row][...] = dot(bases_ref[row - 1].T, work[:, : width(row)])
            send_row(1, row)

    sent = []
    for level in range(1, levels + 1):
        bits = PARTNERS[level - 1]
        last = level == levels
        g_at = width(level) - RANK
        rest = g_at if last or level in HALVED or level == WIDE else g_at - RANK
        wide, narrow, g_cols = slice(rest, None), slice(0, rest), slice(g_at, None)
        ab = both[level]
        sent.append(pending)
        pending = []
        later = list(range(level + 2, levels + 1))
        following = [] if last else [level + 1]
        here = rows_at(offset(level), slice_rows(level))

        def send_part(cols):
            size, start = slice_rows(level), offset(level)
            if level in HALVED and cols is wide:
                size, start = 64, half
            return send(
                ab.at[rows_at(start + RANK, size), cols], ab.at[rows_at(start, size), cols], bits
            )

        def turn(node, rows, first, to):
            for row in rows:
                at = (levels + 1 - row) * RANK
                block = both[node][first : first + RANK, at : at + RANK]
                turned[node][at - RANK : at, to : to + RANK] = block.T

        def settle_coef():
            before = level - 1
            turn(before, range(level + 1, levels + 1), 0, RANK)
            coef[before][...] = dot(core_ref[...], both[before][:, : width(level)])

        def settle():
            old = width(level)
            work[:, :old] = work[:, :old] - dot(work[:, old : old + RANK], coef[level - 1][:RANK])
            turn(level, range(level + 1, levels + 1), RANK, 0)
            if level > 2:
                for copy in sent[level - 2]:
                    copy.wait_send()

        def add_next():
            got_rows[level, level + 1].wait_recv()
            if level == 3:
                got_rows[2, 4].wait_recv()
                kept = mine[3, 4][rows_at(own_part(3), 16), :] + theirs[2, 4][...]
                total[3][rows_at(eighth, 16)] = kept + theirs[3, 4][...]
                return
            total[level][here] = mine[level, level + 1][...] + theirs[level, level + 1][...]

        def gather_next():
            if last:
                return []
            add_next()
            return [gather(total[level], level, slice(None), False)]

        def solve(hooks):
            pairs = [(ab[RANK:, g_cols], ab[:RANK, g_cols])]
            return inverses(pairs, lambda step: hooks.get(step, lambda: None)())[0]

        def core_of(x, ref, into):
            x_t = x.T
            into[:RANK, :RANK] = x
            into[RANK:, RANK:] = x_t
            into[:RANK, RANK:] = -dot(x, ref[:RANK, g_cols])
            into[RANK:, :RANK] = -dot(x_t, ref[RANK:, g_cols])

        if level == WIDE:
            def send_all(cols):
                src = ab.at[rows_at(half + RANK, 64), cols]
                return [
                    send(src, ab.at[rows_at(half, 64), cols], quarters[0]),
                    send(src, both_far.at[rows_at(half + RANK, 64), cols], quarters[1]),
                    send(src, both_far.at[rows_at(half, 64), cols], quarters[2]),
                ]

            def share(copies, cols):
                shared = []
                spots = ((ab, half), (both_far, half + RANK), (both_far, half))
                for copy, (ref, start) in zip(copies, spots):
                    copy.wait_recv()
                    part = ref.at[rows_at(start, 64), cols]
                    shared.append(send(part, part, CORE))
                return shared

            got_wide = send_all(wide)
            got_rest = send_all(narrow)
            settle_coef()
            update_rows(level, following)
            core_wide = share(got_wide, wide)
            settle()
            core_rest = share(got_rest, narrow)
            for copy in core_wide:
                copy.wait_recv()
            core_nine = []

            def add_nine(step):
                if step != 4:
                    return
                for copy in got_nine:
                    copy.wait_recv()
                part = rows_at(half, 64)
                total[level][part] = mine[level, levels][...] + theirs[level, levels][...]
                total_far[part] = nine_far[0] + nine_far[1]
                for ref in (total[level], total_far):
                    core_nine.append(send(ref.at[part], ref.at[part], CORE))

            x, x_far = inverses(
                [
                    (ab[RANK:, g_cols], ab[:RANK, g_cols]),
                    (both_far[RANK:, g_cols], both_far[:RANK, g_cols]),
                ],
                add_nine,
            )
            core_of(x, ab, core_ref)
            core_of(x_far, both_far, core_far)
            for copy in core_rest:
                copy.wait_recv()
            turn(level, [levels], 0, RANK)
            turned_far[:, :RANK] = both_far[RANK:, RANK : 2 * RANK].T
            turned_far[:, RANK:] = both_far[:RANK, RANK : 2 * RANK].T
            left = dot(turned[level][...], core_ref[...])
            left_far = dot(turned_far[...], core_far[...])
            change = dot(left, ab[:, : 2 * RANK])
            change_far = dot(left_far, both_far[:, : 2 * RANK])
            for copy in core_nine:
                copy.wait_recv()
            nine = total[level][...] - change
            nine_other = total_far[...] - change_far
            g_own, g_other = nine[:, RANK:], nine_other[:, RANK:]
            (x,) = inverses([(g_own, g_other)], lambda step: None)
            cols = 2 * RANK
            coef_own = dot(core_ref[:RANK, :], ab[:, :cols])
            after = work[:, :cols] - dot(work[:, cols : cols + RANK], coef_own)
            right = nine_other[:, :RANK] - dot(g_other, nine[:, :RANK])
            out_ref[...] = after[:, :RANK] - dot(after[:, RANK:], dot(x, right))
            break

        got_wide = send_part(wide)
        if level == 1:
            for copy in loads[2:]:
                copy.wait()
            work[:, :RANK] = dot(inv_ref[...], right_ref[...])
            for row in range(levels, 2, -1):
                leaf_work(row)
            ab[RANK:, narrow] = dot(bases_ref[0].T, work[:, narrow])
            got_rest = send_part(narrow)
            leaf_rows(following)
            got_wide.wait_recv()
            x = solve({2: lambda: leaf_rows(later[:1])})
            turn(level, range(2, levels + 1), RANK, 0)
        elif level == 2:
            got_rest = send_part(narrow)
            settle_coef()
            update_rows(level, following)
            got_wide.wait_recv()
            all_wide = gather(ab, level, wide, True)
            leaf_rows(later)
            settle()
            update_rows(level, later)
            finish(all_wide)
            x = solve({})
        else:
            got_rest = send_part(narrow)
            settle_coef()
            update_rows(level, following)
            got_wide.wait_recv()
            all_wide = gather(ab, level, wide, True)
            got_rest.wait_recv()
            held = [gather(ab, level, narrow, False)]
            if level == 4:
                update_rows(level, later)
            if level >= 6:
                settle()
            all_total = gather_next()
            if level != 4:
                update_rows(level, later)
            if level < 6:
                settle()
            finish(all_wide)

            def pass_on():
                held[0] = forward(held[0])

            x = solve({} if level == 4 else {4 if level == 3 else 2: pass_on})
            if level == 5:
                all_total = [forward(part) for part in all_total]

        if last:
            right = ab[:RANK, narrow] - dot(ab[:RANK, g_cols], ab[RANK:, narrow])
            out_ref[...] = work[:, :RANK] - dot(work[:, RANK : 2 * RANK], dot(x, right))
            break

        core_of(x, ab, core_ref)
        if level == 4:
            pass_on()

        def left_side():
            turn(level, [level + 1], 0, RANK)
            return dot(turned[level][g_at - 2 * RANK : g_at - RANK, :], core_ref[...])

        if level not in HALVED:
            left = left_side()
        if level == 1:
            got_rest.wait_recv()
        elif level == 2:
            got_rest.wait_recv()
            all_rest = gather(ab, level, narrow, False)
            relay(later)
            all_total = gather_next()
            finish(all_rest)
        else:
            all_total = [forward(part) for part in all_total]
            if level == WIDE - 1:
                for row in later:
                    got_rows[level, row].wait_recv()
                    summed[row][here] = mine[level, row][...] + theirs[level, row][...]
                    part = summed[row].at[here]
                    spread += [send(part, part, ring) for ring in ring_of(level)]
            finish(held[0])
        if level in HALVED:
            left = left_side()
        change = dot(left, ab[:, : width(level + 1)])
        if level == 1:
            add_next()
        else:
            for part in all_total:
                finish(part)
        both[level + 1][RANK:, :] = total[level][...] - change

    for copy in sum(sent[-1:], []) + pending:
        copy.wait_send()
    assert count[0] == n_sems, count[0]


def shards(right_side, leaf_inverse, bases):
    levels = bases.shape[0]
    n_sems = n_copies(levels)

    def width(level):
        return (levels + 2 - level) * RANK

    def buffer(*shape):
        return pltpu.VMEM(shape, F32)

    scratch = [buffer(right_side.shape[0], width(1))]
    scratch += [buffer(*right_side.shape), buffer(*leaf_inverse.shape), buffer(*bases.shape)]
    for level in range(1, levels + 1):
        scratch.append(buffer(2 * RANK, width(level)))
        if level < levels:
            scratch.append(buffer(2 * RANK, width(level + 1)))
            scratch.append(buffer(width(level + 1) - RANK, 2 * RANK))
            scratch.append(buffer(RANK, width(level + 1)))
        for row in range(level + 1, levels + 1):
            size, next_size = slice_rows(level), slice_rows(level + 1)
            scratch.append(buffer(size, width(row)))
            full = row == level + 1 and level != 3
            size = 16 if level in (2, 3) and row > 3 else size if full else min(size, next_size)
            scratch.append(buffer(size, width(row)))
            if level == 2 and row > 3:
                scratch += [buffer(size, width(row))] * 2
            if level == WIDE - 1 and row > level + 1:
                scratch.append(buffer(RANK, width(row)))
    scratch += [buffer(2 * RANK, 2 * RANK)] * 2
    scratch += [buffer(2 * RANK, 3 * RANK), buffer(RANK, 2 * RANK), buffer(RANK, 2 * RANK)]
    scratch.append(buffer(2, 64, 2 * RANK))
    scratch.append(pltpu.SemaphoreType.DMA((4,)))
    scratch += [pltpu.SemaphoreType.DMA((n_sems,))] * 2
    return pl.pallas_call(
        functools.partial(kernel, levels, n_sems),
        out_shape=jax.ShapeDtypeStruct(right_side.shape, F32),
        in_specs=[pl.BlockSpec(memory_space=pl.ANY)] * 3,
        out_specs=pl.BlockSpec(memory_space=pltpu.VMEM),
        scratch_shapes=scratch,
        compiler_params=pltpu.CompilerParams(
            collective_id=0, has_side_effects=True, vmem_limit_bytes=56 * 2**20
        ),
        name="tree_solve",
    )(right_side, leaf_inverse, bases)


def solution(mesh):
    return jax.shard_map(
        shards,
        mesh=mesh,
        in_specs=(P("leaf", None), P("leaf", None), P(None, "leaf", None)),
        out_specs=P("leaf", None),
        check_vma=False,
    )
```

```python
import functools

import jax
import jax.numpy as jnp
from jax import lax
from jax.experimental import pallas as pl
from jax.experimental.pallas import tpu as pltpu
from jax.sharding import PartitionSpec as P

F32 = jnp.float32
RANK = 128
PARTNERS = ((0,), (1,), (1, 2), (3,), (4,), (5,), (5, 6), (7,), (7, 8))
RING = ((2,), (1, 2), (1,))
CORE = (0,)
AROUND = ((0, 2), (2,), (0, 1, 2), (1, 2), (0, 1), (1,), CORE)
WIDE = 8
HALVED = (3, 4)
STRAIGHT = 8


def dot(a, b):
    return jnp.dot(a, b, precision=lax.Precision.HIGH, preferred_element_type=F32)


def bit(index, b):
    return lax.rem(lax.div(index, 2**b), 2)


def flipped(index, bits):
    for b in bits:
        index = index + (1 - 2 * bit(index, b)) * 2**b
    return index


def chebyshev_heights(count, at):
    heights = [at]
    for _ in range(count):
        heights.append(2 * heights[-1] ** 2 - 1)
    return heights


def inverses(pairs, hook):
    rows = lax.broadcasted_iota(jnp.int32, (RANK, RANK), 0)
    cols = lax.broadcasted_iota(jnp.int32, (RANK, RANK), 1)
    eye = jnp.where(rows == cols, 1.0, 0.0).astype(F32)
    heights = chebyshev_heights(5, 1.25)
    scale = 1.0 / heights[5]
    for height in heights[:5]:
        scale = scale * 2 * height
    qs = [(dot(g_other, g_own), dot(g_own, g_other)) for g_own, g_other in pairs]
    polys = [eye - 0.8 * (eye - q - q_t + dot(q_t, q)) for q, q_t in qs]
    results = [(eye - q_t) * scale for q, q_t in qs]
    for step in range(4):
        hook(step)
        results = [result + dot(poly, result) for poly, result in zip(polys, results)]
        part = 1.0 / heights[step + 1]
        polys = [(1.0 + part) * dot(poly, poly) - part * eye for poly in polys]
    hook(4)
    return [
        result + jnp.dot(poly, result, preferred_element_type=F32)
        for poly, result in zip(polys, results)
    ]


def slice_rows(level):
    if level >= WIDE:
        return 64
    return RANK // min(2 ** (level - 1), 8)


def ring_of(level):
    if level == 2 or level >= WIDE:
        return ()
    return ((1,),) if level == 3 else RING


def around_of(level):
    if level == 2 or level >= WIDE:
        return (CORE,)
    return ((1,), CORE, (0, 1)) if level == 3 else AROUND


def straight(level, first):
    return level >= STRAIGHT or first or ring_of(level) == ()


def n_copies(levels):
    total = 0
    for level in range(1, levels + 1):
        if level == WIDE:
            return total + 17
        total += 2 + levels - level
        if level == 2:
            total += max(levels - 3, 0) + (2 if levels > 2 else 0)
        if level > 1:
            for part in range(2 if level == levels else 3):
                if level in HALVED and part == 0:
                    total += 1
                elif level == 3 and part == 2:
                    total += len(RING) + 1
                elif straight(level, part == 0):
                    total += len(around_of(level))
                else:
                    total += len(ring_of(level)) + 1
            if level == WIDE - 1:
                total += (levels - level - 1) * len(ring_of(level))
    return total


def kernel(levels, n_sems, right_hbm, inv_hbm, bases_hbm, out_ref, work, *scratch):
    def width(level):
        return (levels + 2 - level) * RANK

    scratch = list(scratch)
    right_ref, inv_ref, bases_ref = scratch[:3]
    del scratch[:3]
    both, total = {}, {}
    mine, theirs, coef, turned, summed = {}, {}, {}, {}, {}
    early, relayed = {}, {}
    for level in range(1, levels + 1):
        both[level] = scratch.pop(0)
        if level < levels:
            coef[level] = scratch.pop(0)
            turned[level] = scratch.pop(0)
            total[level] = scratch.pop(0)
        for row in range(level + 1, levels + 1):
            mine[level, row] = scratch.pop(0)
            theirs[level, row] = scratch.pop(0)
            if level == 2 and row > 3:
                early[row], relayed[row] = scratch.pop(0), scratch.pop(0)
            if level == WIDE - 1 and row > level + 1:
                summed[row] = scratch.pop(0)
    core_ref, core_far, both_far, turned_far, total_far, nine_far, load_sem, send_sem, recv_sem = scratch

    loads = []
    for k, (src, dst) in enumerate(
        (
            (inv_hbm, inv_ref),
            (bases_hbm.at[pl.ds(0, 2)], bases_ref.at[pl.ds(0, 2)]),
            (right_hbm, right_ref),
            (bases_hbm.at[pl.ds(2, levels - 2)], bases_ref.at[pl.ds(2, levels - 2)]),
        )
    ):
        loads.append(pltpu.make_async_copy(src, dst, load_sem.at[k]))
        loads[-1].start()

    me = lax.axis_index("leaf")
    core = bit(me, 0)
    low_split = lax.rem(bit(me, 1) + bit(me, 2), 2)
    high_split = bit(me, 2)
    half = 64 * core
    quarter = half + 32 * low_split
    eighth = quarter + 16 * high_split

    def offset(level):
        if level == 1:
            return 0
        if level == 2 or level >= WIDE:
            return half
        return quarter if level == 3 else eighth

    def partner_part(level):
        return {1: 64 * (1 - core), 2: 32 * (1 - low_split), 3: 16 * (1 - high_split)}[level]

    def own_part(level):
        return {1: 64 * core, 2: 32 * low_split, 3: 16 * high_split}[level]

    def rows_at(start, size):
        return pl.ds(start if isinstance(start, int) else pl.multiple_of(start, 16), size)

    count = [0]
    pending = []

    def send(src, dst, bits):
        nonlocal pending
        k = count[0]
        count[0] += 1
        copy = pltpu.make_async_remote_copy(
            src_ref=src,
            dst_ref=dst,
            send_sem=send_sem.at[k],
            recv_sem=recv_sem.at[k],
            device_id=(flipped(me, bits),),
            device_id_type=pl.DeviceIdType.MESH,
        )
        copy.start()
        pending.append(copy)
        return copy

    partners = set(PARTNERS[:levels]) | {CORE}
    for level in range(2, levels + 1):
        partners |= set(around_of(level))
    quarters = ()
    if levels > WIDE:
        near, far = PARTNERS[WIDE - 1 : WIDE + 1]
        quarters = (near, far, tuple(sorted(set(near) ^ set(far))))
    partners = sorted(partners | set(quarters))
    barrier = pltpu.get_barrier_semaphore()
    for bits in partners:
        pl.semaphore_signal(
            barrier, inc=1, device_id=(flipped(me, bits),), device_id_type=pl.DeviceIdType.MESH
        )

    def leaf_work(level):
        at = (levels + 1 - level) * RANK
        work[:, at : at + RANK] = dot(inv_ref[...], bases_ref[level - 1])

    loads[0].wait()
    loads[1].wait()
    leaf_work(1)
    leaf_work(2)
    top = width(1) - 2 * RANK
    both[1][RANK:, top:] = dot(bases_ref[0].T, work[:, top:])

    pl.semaphore_wait(barrier, len(partners))

    def gather(ref, level, cols, first):
        ahead = level == 3 and ref is not both[3]
        whole = straight(level, first)
        here = rows_at(eighth, 16) if ahead else rows_at(offset(level), slice_rows(level))
        if first and level in HALVED:
            here = rows_at(half, 64)
            return (ref, cols, [send(ref.at[here, cols], ref.at[here, cols], CORE)], True)
        here = ref.at[here, cols]
        ring = RING if ahead else ring_of(level)
        copies = [send(here, here, bits) for bits in (around_of(level) if whole else ring)]
        return (ref, cols, copies, whole)

    def forward(started):
        ref, cols, copies, whole = started
        if whole:
            return started
        for copy in copies:
            copy.wait_recv()
        here = ref.at[rows_at(half, 64), cols]
        return (ref, cols, [send(here, here, CORE)], True)

    def finish(started):
        for copy in started[2]:
            copy.wait_recv()

    got_rows, got_early = {}, {}
    spread, got_nine, got_halves = [], [], []

    def send_row(level, row):
        size, next_size = slice_rows(level), slice_rows(level + 1)
        src = mine[level, row]
        if level == WIDE:
            for way, dst in zip(quarters, (theirs[level, row], nine_far.at[0], nine_far.at[1])):
                got_nine.append(send(src, dst, way))
            return
        if level == 2 and row == 3:
            cut = width(row) // (2 * RANK) * RANK
            for cols in (slice(0, cut), slice(cut, width(row))):
                copy = send(src.at[:, cols], theirs[2, 3].at[:, cols], PARTNERS[1])
                got_halves.append((cols, copy))
            return
        if level == 2 and row > 3:
            part = rows_at(32 * (1 - low_split) + 16 * (1 - high_split), 16)
            got_early[row] = send(src.at[part], early[row], PARTNERS[2])
            return
        if (row > level + 1 or level == 3) and next_size < size:
            src = src.at[rows_at(partner_part(level), next_size)]
        got_rows[level, row] = send(src, theirs[level, row], PARTNERS[level - 1])

    def relay(rows):
        for row in rows:
            got_early[row].wait_recv()
            part = rows_at(32 * (1 - low_split) + 16 * high_split, 16)
            relayed[row][...] = mine[2, row][part, :] + early[row][...]
            got_rows[2, row] = send(relayed[row], theirs[2, row], PARTNERS[1])

    def update_rows(level, rows):
        if not rows:
            return
        before, size = level - 1, slice_rows(level)
        left = []
        for row in rows:
            at = (levels - row) * RANK
            left.append(turned[before][rows_at(at + offset(level), size), :])
        left = left[0] if len(left) == 1 else jnp.concatenate(left, axis=0)
        change = dot(left, coef[before][:, : width(rows[0])])
        for i, row in enumerate(rows):
            if row in summed and level == WIDE:
                while spread:
                    spread.pop().wait_recv()
                base = summed[row][rows_at(half, 64), :]
            else:
                base = mine[before, row]
                if size < slice_rows(before):
                    base = base.at[rows_at(own_part(before), size)]
                base = base[...]
                for node in {2: (), 3: (2, 3)}.get(before, (before,)):
                    got_rows[node, row].wait_recv()
                    base = base + theirs[node, row][...]
            mine[level, row][...] = base - change[i * size : (i + 1) * size, : width(row)]
            send_row(level, row)

    def leaf_rows(rows):
        for row in rows:
            mine[1, row][...] = dot(bases_ref[row - 1].T, work[:, : width(row)])
            send_row(1, row)

    sent = []
    for level in range(1, levels + 1):
        bits = PARTNERS[level - 1]
        last = level == levels
        g_at = width(level) - RANK
        rest = g_at if last or level in HALVED or level == WIDE else g_at - RANK
        wide, narrow, g_cols = slice(rest, None), slice(0, rest), slice(g_at, None)
        ab = both[level]
        sent.append(pending)
        pending = []
        later = list(range(level + 2, levels + 1))
        following = [] if last else [level + 1]
        here = rows_at(offset(level), slice_rows(level))

        def send_part(cols):
            size, start = slice_rows(level), offset(level)
            if level in HALVED and cols is wide:
                size, start = 64, half
            return send(
                ab.at[rows_at(start + RANK, size), cols], ab.at[rows_at(start, size), cols], bits
            )

        def turn(node, rows, first, to):
            for row in rows:
                at = (levels + 1 - row) * RANK
                block = both[node][first : first + RANK, at : at + RANK]
                turned[node][at - RANK : at, to : to + RANK] = block.T

        def settle_coef():
            before = level - 1
            turn(before, range(level + 1, levels + 1), 0, RANK)
            coef[before][...] = dot(core_ref[...], both[before][:, : width(level)])

        def settle():
            old = width(level)
            work[:, :old] = work[:, :old] - dot(work[:, old : old + RANK], coef[level - 1][:RANK])
            turn(level, range(level + 1, levels + 1), RANK, 0)
            if level > 2:
                for copy in sent[level - 2]:
                    copy.wait_send()

        def add_next():
            got_rows[level, level + 1].wait_recv()
            if level == 3:
                got_rows[2, 4].wait_recv()
                kept = mine[3, 4][rows_at(own_part(3), 16), :] + theirs[2, 4][...]
                total[3][rows_at(eighth, 16)] = kept + theirs[3, 4][...]
                return
            total[level][here] = mine[level, level + 1][...] + theirs[level, level + 1][...]

        def gather_next():
            if last:
                return []
            if level == 2:
                parts = []
                for cols, copy in got_halves:
                    copy.wait_recv()
                    total[2][here, cols] = mine[2, 3][:, cols] + theirs[2, 3][:, cols]
                    parts.append(gather(total[2], 2, cols, False))
                return parts
            add_next()
            return [gather(total[level], level, slice(None), False)]

        def solve(hooks):
            pairs = [(ab[RANK:, g_cols], ab[:RANK, g_cols])]
            return inverses(pairs, lambda step: hooks.get(step, lambda: None)())[0]

        def core_of(x, ref, into):
            x_t = x.T
            into[:RANK, :RANK] = x
            into[RANK:, RANK:] = x_t
            into[:RANK, RANK:] = -dot(x, ref[:RANK, g_cols])
            into[RANK:, :RANK] = -dot(x_t, ref[RANK:, g_cols])

        if level == WIDE:
            def send_all(cols):
                src = ab.at[rows_at(half + RANK, 64), cols]
                return [
                    send(src, ab.at[rows_at(half, 64), cols], quarters[0]),
                    send(src, both_far.at[rows_at(half + RANK, 64), cols], quarters[1]),
                    send(src, both_far.at[rows_at(half, 64), cols], quarters[2]),
                ]

            def share(copies, cols):
                shared = []
                spots = ((ab, half), (both_far, half + RANK), (both_far, half))
                for copy, (ref, start) in zip(copies, spots):
                    copy.wait_recv()
                    part = ref.at[rows_at(start, 64), cols]
                    shared.append(send(part, part, CORE))
                return shared

            got_wide = send_all(wide)
            got_rest = send_all(narrow)
            settle_coef()
            update_rows(level, following)
            core_wide = share(got_wide, wide)
            settle()
            core_rest = share(got_rest, narrow)
            for copy in core_wide:
                copy.wait_recv()
            core_nine = []

            def add_nine(step):
                if step != 4:
                    return
                for copy in got_nine:
                    copy.wait_recv()
                part = rows_at(half, 64)
                total[level][part] = mine[level, levels][...] + theirs[level, levels][...]
                total_far[part] = nine_far[0] + nine_far[1]
                for ref in (total[level], total_far):
                    core_nine.append(send(ref.at[part], ref.at[part], CORE))

            x, x_far = inverses(
                [
                    (ab[RANK:, g_cols], ab[:RANK, g_cols]),
                    (both_far[RANK:, g_cols], both_far[:RANK, g_cols]),
                ],
                add_nine,
            )
            core_of(x, ab, core_ref)
            core_of(x_far, both_far, core_far)
            for copy in core_rest:
                copy.wait_recv()
            turn(level, [levels], 0, RANK)
            turned_far[:, :RANK] = both_far[RANK:, RANK : 2 * RANK].T
            turned_far[:, RANK:] = both_far[:RANK, RANK : 2 * RANK].T
            left = dot(turned[level][...], core_ref[...])
            left_far = dot(turned_far[...], core_far[...])
            change = dot(left, ab[:, : 2 * RANK])
            change_far = dot(left_far, both_far[:, : 2 * RANK])
            for copy in core_nine:
                copy.wait_recv()
            nine = total[level][...] - change
            nine_other = total_far[...] - change_far
            g_own, g_other = nine[:, RANK:], nine_other[:, RANK:]
            (x,) = inverses([(g_own, g_other)], lambda step: None)
            cols = 2 * RANK
            coef_own = dot(core_ref[:RANK, :], ab[:, :cols])
            after = work[:, :cols] - dot(work[:, cols : cols + RANK], coef_own)
            right = nine_other[:, :RANK] - dot(g_other, nine[:, :RANK])
            out_ref[...] = after[:, :RANK] - dot(after[:, RANK:], dot(x, right))
            break

        got_wide = send_part(wide)
        if level == 1:
            for copy in loads[2:]:
                copy.wait()
            work[:, :RANK] = dot(inv_ref[...], right_ref[...])
            for row in range(levels, 2, -1):
                leaf_work(row)
            ab[RANK:, narrow] = dot(bases_ref[0].T, work[:, narrow])
            got_rest = send_part(narrow)
            leaf_rows(following)
            got_wide.wait_recv()
            x = solve({2: lambda: leaf_rows(later[:1])})
            turn(level, range(2, levels + 1), RANK, 0)
        elif level == 2:
            got_rest = send_part(narrow)
            settle_coef()
            update_rows(level, following)
            got_wide.wait_recv()
            all_wide = gather(ab, level, wide, True)
            leaf_rows(later)
            settle()
            update_rows(level, later)
            finish(all_wide)
            x = solve({})
        else:
            got_rest = send_part(narrow)
            settle_coef()
            update_rows(level, following)
            got_wide.wait_recv()
            all_wide = gather(ab, level, wide, True)
            got_rest.wait_recv()
            held = [gather(ab, level, narrow, False)]
            if level == 4:
                update_rows(level, later)
            if level >= 6:
                settle()
            all_total = gather_next()
            if level != 4:
                update_rows(level, later)
            if level < 6:
                settle()
            finish(all_wide)

            def pass_on():
                held[0] = forward(held[0])

            x = solve({} if level == 4 else {4 if level == 3 else 2: pass_on})
            if level == 5:
                all_total = [forward(part) for part in all_total]

        if last:
            right = ab[:RANK, narrow] - dot(ab[:RANK, g_cols], ab[RANK:, narrow])
            out_ref[...] = work[:, :RANK] - dot(work[:, RANK : 2 * RANK], dot(x, right))
            break

        core_of(x, ab, core_ref)
        if level == 4:
            pass_on()

        def left_side():
            turn(level, [level + 1], 0, RANK)
            return dot(turned[level][g_at - 2 * RANK : g_at - RANK, :], core_ref[...])

        if level not in HALVED:
            left = left_side()
        if level == 1:
            got_rest.wait_recv()
        elif level == 2:
            got_rest.wait_recv()
            all_rest = gather(ab, level, narrow, False)
            relay(later)
            all_total = gather_next()
            finish(all_rest)
        else:
            all_total = [forward(part) for part in all_total]
            if level == WIDE - 1:
                for row in later:
                    got_rows[level, row].wait_recv()
                    summed[row][here] = mine[level, row][...] + theirs[level, row][...]
                    part = summed[row].at[here]
                    spread += [send(part, part, ring) for ring in ring_of(level)]
            finish(held[0])
        if level in HALVED:
            left = left_side()
        change = dot(left, ab[:, : width(level + 1)])
        if level == 1:
            add_next()
        else:
            for part in all_total:
                finish(part)
        both[level + 1][RANK:, :] = total[level][...] - change

    for copy in sum(sent[-1:], []) + pending:
        copy.wait_send()
    assert count[0] == n_sems, count[0]


def shards(right_side, leaf_inverse, bases):
    levels = bases.shape[0]
    n_sems = n_copies(levels)

    def width(level):
        return (levels + 2 - level) * RANK

    def buffer(*shape):
        return pltpu.VMEM(shape, F32)

    scratch = [buffer(right_side.shape[0], width(1))]
    scratch += [buffer(*right_side.shape), buffer(*leaf_inverse.shape), buffer(*bases.shape)]
    for level in range(1, levels + 1):
        scratch.append(buffer(2 * RANK, width(level)))
        if level < levels:
            scratch.append(buffer(2 * RANK, width(level + 1)))
            scratch.append(buffer(width(level + 1) - RANK, 2 * RANK))
            scratch.append(buffer(RANK, width(level + 1)))
        for row in range(level + 1, levels + 1):
            size, next_size = slice_rows(level), slice_rows(level + 1)
            scratch.append(buffer(size, width(row)))
            full = row == level + 1 and level != 3
            size = 16 if level in (2, 3) and row > 3 else size if full else min(size, next_size)
            scratch.append(buffer(size, width(row)))
            if level == 2 and row > 3:
                scratch += [buffer(size, width(row))] * 2
            if level == WIDE - 1 and row > level + 1:
                scratch.append(buffer(RANK, width(row)))
    scratch += [buffer(2 * RANK, 2 * RANK)] * 2
    scratch += [buffer(2 * RANK, 3 * RANK), buffer(RANK, 2 * RANK), buffer(RANK, 2 * RANK)]
    scratch.append(buffer(2, 64, 2 * RANK))
    scratch.append(pltpu.SemaphoreType.DMA((4,)))
    scratch += [pltpu.SemaphoreType.DMA((n_sems,))] * 2
    return pl.pallas_call(
        functools.partial(kernel, levels, n_sems),
        out_shape=jax.ShapeDtypeStruct(right_side.shape, F32),
        in_specs=[pl.BlockSpec(memory_space=pl.ANY)] * 3,
        out_specs=pl.BlockSpec(memory_space=pltpu.VMEM),
        scratch_shapes=scratch,
        compiler_params=pltpu.CompilerParams(
            collective_id=0, has_side_effects=True, vmem_limit_bytes=56 * 2**20
        ),
        name="tree_solve",
    )(right_side, leaf_inverse, bases)


def solution(mesh):
    return jax.shard_map(
        shards,
        mesh=mesh,
        in_specs=(P("leaf", None), P("leaf", None), P(None, "leaf", None)),
        out_specs=P("leaf", None),
        check_vma=False,
    )
```
